128 devices in a mesh: group: 4 (over x), shard: 32 (over y, z, core).
Axes of the slice: x: 4, y: 4, z: 4, core: 2. Of those that a mesh axis runs over, the one named last changes fastest.
Arguments:
- queries: float32 [1024, 768], P(('group', 'shard')), may hold values from -6 to 6
- codebook: float32 [96, 256, 8], replicated, may hold values from -0.21875 to 0.21875
- pq_codes: int32 [1024, 96, 256], P(('group', 'shard')), may hold values from 0 to 255
- probes: int32 [1024, 8], P('group'), may hold values from 0 to 255, all different within a row
- vectors: float32 [131072, 768], P(('group', 'shard')), may hold values from -0.21875 to 0.21875
- cand_owner: int32 [1024, 16], P(('group', 'shard')), may hold values from 0 to 127, all different within a row; in each aligned block of 8 rows (0 to 7, 8 to 15, ...) at most 2 rows name the same one
- cand_row: int32 [1024, 16], P(('group', 'shard')), may hold values from 0 to 1023
Outputs:
- pq_scores: float32 [1024, 256, 256], P(('group', 'shard'))
- rerank_scores: float32 [1024, 16], P(('group', 'shard'))
The draws below stay inside these ranges and needn't reach their ends.
Inputs may be any that keep to these rules, and one draw needn't show every extreme that they name: The 8 probes of one query are distinct. `cand_owner`: the 16 owners of one query are distinct. Among the queries of one device no owner appears more than 2 times, and some owner appears exactly 2 times.
All inputs are finite; a program needn't handle non-finite values.
Results may differ from the reference program's by a relative error of at most 0.0029.
Values may be sent and summed in bfloat16 or wider, within the bound.
A program may use at most 128 MiB of HBM per device.

```python
import math
import jax
import jax.numpy as jnp
import numpy as np
from jax import lax

M = 96
DS = 8
D = 768
KS = 256
P_SIZE = 8
C = 16
LIST_LEN = 256
Q_DEV = 8
VEC_DEV = 1024
OWNERS = 128
GROUP_Q = 256
QUERIES = 1024
LISTS_G = 256
LISTS = 1024
VECS = 131072
CAP = 2


def plant(array, rng, low, high):
    longest = array.shape.index(max(array.shape))
    spots = []
    for shift in (0, 1):
        where = [jax.random.randint(jax.random.fold_in(rng, axis), (), 0, length) for axis, length in enumerate(array.shape)]
        where[longest] = (where[longest] + shift) % array.shape[longest]
        spots.append(tuple(where))
    return array.at[spots[0]].set(low).at[spots[1]].set(high)


def steps_of(key, extent, split, smallest, top_value):
    level, own = 1.0, jax.random.fold_in(key, 6)
    for axis_at, blocks in split:
        heights = jnp.exp(jax.random.uniform(jax.random.fold_in(own, axis_at), (blocks,), jnp.float32, smallest / len(split), top_value / len(split)))
        level = level * jnp.repeat(heights, extent[axis_at] // blocks).reshape([-1 if axis == axis_at else 1 for axis in range(len(extent))])
    return level


def distinct(key, rows, number_of, top, lift):
    sequence = jax.random.permutation(jax.random.fold_in(key, 1), number_of)
    favour = sequence
    for power in range(3):
        favour = favour * favour // number_of
    favour = favour * lift // number_of
    tickets = jax.random.randint(jax.random.fold_in(key, 2), (rows, number_of), 0, 4096) + favour
    holders = jax.random.permutation(jax.random.fold_in(key, 3), rows)[jnp.arange(number_of) % rows]
    tickets = jnp.where(jnp.arange(rows)[:, None] == holders[None, :], 1 << 14, tickets)
    merit = tickets * number_of + jnp.arange(number_of)
    return lax.top_k(merit.astype(jnp.int32), top)[1].astype(jnp.int32)


def assign_block(own_key, own, number, rows, number_of, top, bound, skew):
    order = jax.random.permutation(own_key, number_of)
    packed, ordinary = portions_of(number_of, rows * top, bound, skew, True), portions_of(number_of, rows * top, bound, skew, False)
    places = jnp.arange(number_of)

    def named(lengths, turn):
        used = int((lengths > 0).sum())
        fixed = max(1, used // 4)
        shifted = fixed + (places - fixed + turn * (used - fixed)) % max(1, number_of - fixed)
        return jnp.zeros((number_of,), jnp.int32).at[order[jnp.where(places < fixed, places, shifted)]].set(jnp.asarray(lengths, jnp.int32))

    lengths = jnp.where(number % 4 == 0, named(packed, number // 4), named(ordinary, number - number // 4 - 1))
    mixed = jax.random.permutation(jax.random.fold_in(own, 3), number_of)
    source_of, sink = mixed[0:number_of // 2 * 2:2], mixed[1:number_of // 2 * 2:2]
    margin = jnp.minimum(lengths[source_of] - 1, bound - lengths[sink]) // 2
    margin = jnp.where((source_of == order[0]) | (sink == order[0]) | (lengths[sink] == 0), 0, jnp.maximum(margin, 0))
    shifted = jax.random.randint(jax.random.fold_in(own, 4), (number_of // 2,), 0, 1 << 20) % (margin + 1)
    lengths = lengths.at[source_of].add(-shifted).at[sink].add(shifted)
    labels = jnp.searchsorted(jnp.cumsum(lengths), jnp.arange(rows * top), side="right").astype(jnp.int32)
    grid = labels.reshape(top, rows).T
    grid = grid[jax.random.permutation(jax.random.fold_in(own, 1), rows)]
    turn = jax.random.randint(jax.random.fold_in(own, 2), (rows, 1), 0, top)
    return jnp.take_along_axis(grid, (jnp.arange(top)[None, :] + turn) % top, axis=1)


def portions_of(number_of, total, limit, lean, full):
    loads = [(1 << 20) // math.isqrt(standing ** lean) + 1 for standing in range(1, number_of + 1)]
    largest = limit if full else min(limit, max(-(-total // number_of), total * loads[0] // sum(loads)))
    least = 1 if total - largest >= number_of - 1 else 0
    given, rest = [largest] + [least] * (number_of - 1), total - largest - least * (number_of - 1)
    while rest > 0:
        free = [i for i in range(1, number_of) if given[i] < largest] or [i for i in range(1, number_of) if given[i] < limit]
        pool, budget = sum([loads[i] for i in free]), rest
        for i in free:
            extra = min(limit - given[i], max(1, budget * loads[i] // pool), rest)
            given[i] = given[i] + extra
            rest = rest - extra
    return np.array(given)


def bell_draw(own_key, dims, spread, reach, split=(), kind=jnp.bfloat16):
    entries = jax.random.normal(own_key, dims, jnp.float32) * spread
    if len(split) > 0:
        entries = steps_of(own_key, dims, split, -0.22, 0.18) * entries
    return jnp.clip(entries, min=-reach, max=reach).astype(kind)


def setup_inputs(seed: int = 0) -> dict:
    streams_of = jax.random.split(jax.random.key(seed), 8)
    queries = bell_draw(streams_of[0], (QUERIES, D), 1.0, 6.0, ((0, 128),), jnp.float32)
    codebook = bell_draw(streams_of[1], (M, KS, DS), D ** -0.5, 0.21875, (), jnp.float32)
    pq_codes = plant(jax.random.randint(streams_of[2], (LISTS, M, LIST_LEN), 0, KS), jax.random.fold_in(streams_of[2], 1), 0, KS - 1).astype(jnp.int32)
    probes = distinct(streams_of[3], QUERIES, LISTS_G, P_SIZE, 512)
    vectors = bell_draw(streams_of[4], (VECS, D), D ** -0.5, 0.21875, ((0, 128),), jnp.float32)
    cand_owner_keys = jax.random.split(jax.random.fold_in(streams_of[5], 1), QUERIES // Q_DEV)
    cand_owner_turns = jax.random.permutation(jax.random.fold_in(streams_of[5], 3), QUERIES // Q_DEV)
    cand_owner = jax.vmap(lambda own, number: assign_block(jax.random.fold_in(streams_of[5], 2), own, number, Q_DEV, OWNERS, C, CAP, 2))(cand_owner_keys, cand_owner_turns).reshape((QUERIES, C))
    cand_row = plant(jax.random.randint(streams_of[6], (QUERIES, C), 0, VEC_DEV), jax.random.fold_in(streams_of[6], 1), 0, VEC_DEV - 1).astype(jnp.int32)
    return {"queries": queries, "codebook": codebook, "pq_codes": pq_codes, "probes": probes, "vectors": vectors, "cand_owner": cand_owner, "cand_row": cand_row}


def reference(queries, codebook, pq_codes, probes, vectors, cand_owner, cand_row):
    number = queries.shape[0]
    tables = jnp.einsum("qmd,mkd->qmk", queries.reshape(number, M, DS), codebook, precision=lax.Precision.HIGHEST).astype(jnp.bfloat16)
    positions = jnp.arange(number, dtype=jnp.int32)
    group_of = positions // GROUP_Q
    within = positions % GROUP_Q
    chosen_lists = (probes + (group_of * LISTS_G)[:, None]).astype(jnp.int32)
    centre = jnp.arange(M, dtype=jnp.int32)

    def one_query(inputs):
        query_table, chosen = inputs
        picked = pq_codes[chosen]
        values = query_table[centre[None, :, None], picked].astype(jnp.float32)
        return jnp.sum(values, axis=1)

    totals = lax.map(one_query, (tables, chosen_lists))
    pq_scores = jnp.zeros((LISTS, LIST_LEN, GROUP_Q), jnp.float32)
    pq_scores = pq_scores.at[chosen_lists[:, :, None], jnp.arange(LIST_LEN, dtype=jnp.int32)[None, None, :], within[:, None, None]].set(totals)
    global_ids = (cand_owner * VEC_DEV + cand_row).astype(jnp.int32)
    found = vectors[global_ids]
    exact_scores = jnp.einsum("qd,qcd->qc", queries, found, precision=lax.Precision.HIGHEST)
    return pq_scores, exact_scores
```

```python
import jax
import jax.numpy as jnp
from jax import lax
from jax.experimental import pallas as pl
from jax.experimental.pallas import tpu as pltpu
from jax.sharding import PartitionSpec as P

MESH = pl.DeviceIdType.MESH
F32, BF16, I32 = jnp.float32, jnp.bfloat16, jnp.int32


def lane_gather(table, index):
    numbers = lax.GatherDimensionNumbers(
        offset_dims=(),
        collapsed_slice_dims=(1,),
        start_index_map=(1,),
        operand_batching_dims=(0,),
        start_indices_batching_dims=(0,),
    )
    return lax.gather(
        table, index[..., None], numbers, (1, 1), mode=lax.GatherScatterMode.PROMISE_IN_BOUNDS
    )


def iota(shape, dim):
    return lax.broadcasted_iota(I32, shape, dim)


def kernel(
    q_ref,
    probes_ref,
    owner_ref,
    row_ref,
    codes_hbm,
    book_hbm,
    vectors_hbm,
    pq_ref,
    rr_ref,
    codes,
    book,
    vectors,
    book16,
    vectors16,
    decoded,
    group_q,
    cube_q,
    cube_want,
    want_t,
    want_out,
    want_in,
    slot_out,
    slot_in,
    score_out,
    score_in,
    spread,
    back,
    total,
    load_sem,
    cq_s, cq_r, cw_s, cw_r,
    g_s, g_r,
    sq_s, sq_r, sw_s, sw_r,
    rs_s, rs_r, bk_s, bk_r,
):
    x = lax.axis_index("group")
    s = lax.axis_index("shard")
    y, z, c = s // 8, (s // 2) % 4, s % 2
    a = x * 2 + c
    w = y * 4 + z

    def device(x, y, z, c):
        return {"group": x, "shard": (y * 4 + z) * 2 + c}

    def cube_peer(i):
        p = (a + i) % 8
        return p, device(p // 2, y, z, p % 2)

    def plane_peer(i):
        p = (w + i) % 16
        return p, device(x, p // 4, p % 4, c)

    loads = [
        pltpu.make_async_copy(src, dst, load_sem.at[i])
        for i, (src, dst) in enumerate(
            ((book_hbm, book), (codes_hbm, codes), (vectors_hbm, vectors))
        )
    ]
    for load in loads:
        load.start()

    barrier = pltpu.get_barrier_semaphore()
    for i in range(1, 8):
        pl.semaphore_signal(barrier, inc=1, device_id=cube_peer(i)[1], device_id_type=MESH)
    for i in range(1, 16):
        pl.semaphore_signal(barrier, inc=1, device_id=plane_peer(i)[1], device_id_type=MESH)

    def remote(src, dst, send, recv, to):
        return pltpu.make_async_remote_copy(
            src_ref=src, dst_ref=dst, send_sem=send, recv_sem=recv, device_id=to, device_id_type=MESH
        )

    q = q_ref[...]
    high = q.astype(BF16)
    low = (q - high.astype(F32)).astype(BF16)
    cube_q[a] = jnp.concatenate([high[:, :384], high[:, 384:]], axis=0)
    for h in range(2):
        group_q[h, y, z, c] = jnp.concatenate(
            [high[:, h * 384 : h * 384 + 384], low[:, h * 384 : h * 384 + 384]], axis=0
        )
    owner = owner_ref[...]
    row = row_ref[...].astype(F32)
    lanes = iota((8, 128), 1)
    present = jnp.zeros((8, 128), F32)
    wanted = jnp.zeros((8, 128), F32)
    for k in range(16):
        hit = owner[:, k : k + 1] == lanes
        present = jnp.where(hit, 1.0, present)
        wanted = jnp.where(hit, row[:, k : k + 1], wanted)
    earlier = (iota((8, 8), 1) < iota((8, 8), 0)).astype(BF16)
    rank = jnp.dot(earlier, present.astype(BF16), preferred_element_type=F32)
    slot = (a * 2).astype(F32) + rank
    cube_want[a] = jnp.where(present > 0.0, slot * 1024.0 + wanted, -1.0)
    spread[...] = jnp.zeros((128, 128), F32)

    pl.semaphore_wait(barrier, 22)

    cube_copies = []
    for i in range(1, 8):
        _, to = cube_peer(i)
        for copy in (
            remote(cube_q.at[a], cube_q.at[a], cq_s.at[i], cq_r.at[i], to),
            remote(cube_want.at[a], cube_want.at[a], cw_s.at[i], cw_r.at[i], to),
        ):
            copy.start()
            cube_copies.append(copy)

    def line_peer(axis, i):
        return (
            device(x, (y + i) % 4, z, c) if axis == 0 else device(x, y, (z + i) % 4, c)
        )

    first_copies, second_copies = [], []
    for i in (1, 3, 2):
        for h in range(2):
            block = group_q.at[h, y, z, c]
            copy = remote(block, block, g_s.at[h, 0, i], g_r.at[h, 0, i], line_peer(h, i))
            copy.start()
            first_copies.append(copy)

    loads[0].wait()

    def to_book16(i, _):
        pair = book[pl.ds(i * 2, 2)]
        book16[i] = jnp.concatenate([pair[0], pair[1]], axis=0).astype(BF16)
        return 0

    lax.fori_loop(0, 48, to_book16, 0, unroll=8)
    loads[1].wait()

    def decode(l, _):
        for m in range(48):
            for h in range(2):
                span = slice(h * 128, h * 128 + 128)
                index = jnp.concatenate(
                    [
                        jnp.broadcast_to(codes[l, 2 * m : 2 * m + 1, span], (8, 128)),
                        jnp.broadcast_to(codes[l, 2 * m + 1 : 2 * m + 2, span], (8, 128)),
                    ],
                    axis=0,
                )
                near = (index & 127).astype(jnp.int16)
                decoded[l, m * 16 : m * 16 + 16, span] = jnp.where(
                    index < 128,
                    lane_gather(book16[m, :, :128], near),
                    lane_gather(book16[m, :, 128:], near),
                )
        return 0

    lax.fori_loop(0, 2, decode, 0)

    for copy in cube_copies:
        copy.wait_recv()
    wants = jnp.concatenate(
        [cube_want[...].reshape(64, 128), jnp.full((64, 128), -1.0, F32)], axis=0
    )
    want_t[...] = wants.T.astype(I32)
    places = iota((16, 128), 0)
    picks = []
    for p in range(16):
        line = want_t[pl.ds(x * 32 + p * 2 + c, 1), :]
        want_out[p] = line
        picks.append(
            jnp.where((jnp.broadcast_to(line, (16, 128)) >> 10) == places, 1.0, 0.0)
        )
    pick = jnp.concatenate(picks, axis=0)[:, :64].astype(BF16)
    cube = cube_q[...]
    for h in range(2):
        columns = cube[:, h * 8 : h * 8 + 8, :].reshape(64, 384)
        chosen = jnp.dot(pick, columns, preferred_element_type=F32).astype(BF16)
        slot_out[:, :, h * 384 : h * 384 + 384] = chosen.reshape(16, 16, 384)
    slot_in[w] = slot_out[w]
    want_in[w] = want_out[w]
    slot_copies = []
    for i in range(1, 16):
        p, to = plane_peer(i)
        for copy in (
            remote(slot_out.at[p], slot_in.at[w], sq_s.at[i], sq_r.at[i], to),
            remote(want_out.at[p], want_in.at[w], sw_s.at[i], sw_r.at[i], to),
        ):
            copy.start()
            slot_copies.append(copy)

    for copy in first_copies:
        copy.wait_recv()
    for i in (1, 3, 2):
        for h in range(2):
            block = group_q.at[h, :, z, c] if h == 0 else group_q.at[h, y, :, c]
            copy = remote(block, block, g_s.at[h, 1, i], g_r.at[h, 1, i], line_peer(1 - h, i))
            copy.start()
            second_copies.append(copy)

    lax.fori_loop(2, 5, decode, 0)
    loads[2].wait()

    def to_vectors16(i, _):
        span = pl.ds(pl.multiple_of(i * 128, 128), 128)
        vectors16[span, :] = vectors[span, :].astype(BF16)
        return 0

    lax.fori_loop(0, 8, to_vectors16, 0)

    for copy in second_copies:
        copy.wait_recv()
    sibling = device(x, y, z, 1 - c)
    core_copies = []
    for h in range(2):
        block = group_q.at[h, :, :, c]
        copy = remote(block, block, g_s.at[h, 2, 0], g_r.at[h, 2, 0], sibling)
        copy.start()
        core_copies.append(copy)

    lax.fori_loop(5, 8, decode, 0)

    for copy in slot_copies:
        copy.wait_recv()
    slots = slot_in[...].reshape(256, 768)
    ids = []
    for p in range(16):
        line = jnp.broadcast_to(want_in[p], (16, 128))
        ids.append(jnp.where((line >> 10) == places, line & 1023, 0))
    ids = jnp.sum(jnp.concatenate(ids, axis=0).astype(F32), axis=1, keepdims=True).astype(I32)
    found = jnp.zeros((256, 256), F32)
    for b in range(4):
        part = lax.dot_general(
            slots,
            vectors16[b * 256 : b * 256 + 256, :],
            (((1,), (1,)), ((), ())),
            preferred_element_type=F32,
        )
        found = jnp.where(iota((256, 256), 1) + b * 256 == ids, part, found)
        if b == 0:
            found = jnp.where(iota((256, 256), 1) == ids, part, 0.0)
    scored = jnp.sum(found, axis=1, keepdims=True)
    for p in range(16):
        mine = jnp.broadcast_to(scored[p * 16 : p * 16 + 16, :], (16, 128))
        score_out[p] = jnp.sum(
            jnp.where(iota((16, 128), 1) == places, mine, 0.0), axis=0, keepdims=True
        )
    score_in[w] = score_out[w]
    score_copies = []
    for i in range(1, 16):
        p, to = plane_peer(i)
        copy = remote(score_out.at[p], score_in.at[w], rs_s.at[i], rs_r.at[i], to)
        copy.start()
        score_copies.append(copy)

    for copy in core_copies:
        copy.wait_recv()

    probes = probes_ref[...]

    def score_list(l, _):
        left = jnp.concatenate(
            [group_q[0].reshape(512, 384), group_q[1].reshape(512, 384)], axis=1
        )
        both = jnp.dot(left, decoded[l], preferred_element_type=F32).reshape(32, 2, 8, 256)
        sums = (both[:, 0] + both[:, 1]).reshape(256, 256)
        probed = jnp.max(jnp.where(probes == s * 8 + l, 1.0, 0.0), axis=0, keepdims=True)
        pq_ref[l] = jnp.where(probed > 0.0, sums.T, 0.0)
        return 0

    lax.fori_loop(0, 4, score_list, 0)

    for copy in score_copies:
        copy.wait_recv()
    for p in range(16):
        spread[pl.ds(x * 32 + p * 2 + c, 1), :] = score_in[p]
    back[a] = spread[...].T[:16, :]
    back_copies = []
    for i in range(1, 8):
        _, to = cube_peer(i)
        copy = remote(back.at[a], back.at[a], bk_s.at[i], bk_r.at[i], to)
        copy.start()
        back_copies.append(copy)

    lax.fori_loop(4, 8, score_list, 0)

    for copy in back_copies:
        copy.wait_recv()
    total[...] = jnp.sum(back[...], axis=0)
    own = jnp.where(rank < 0.5, total[pl.ds(a * 2, 1), :], total[pl.ds(a * 2 + 1, 1), :])
    result = jnp.zeros((8, 16), F32)
    for k in range(16):
        value = jnp.sum(
            jnp.where(owner[:, k : k + 1] == lanes, own, 0.0), axis=1, keepdims=True
        )
        result = jnp.where(iota((8, 16), 1) == k, value, result)
    rr_ref[...] = result

    for copy in (
        cube_copies + first_copies + second_copies + core_copies
        + slot_copies + score_copies + back_copies
    ):
        copy.wait_send()


def per_device(queries, codebook, pq_codes, probes, vectors, cand_owner, cand_row):
    vmem = pl.BlockSpec(memory_space=pltpu.VMEM)
    hbm = pl.BlockSpec(memory_space=pl.ANY)
    dma = pltpu.SemaphoreType.DMA
    return pl.pallas_call(
        kernel,
        out_shape=(
            jax.ShapeDtypeStruct((8, 256, 256), F32),
            jax.ShapeDtypeStruct((8, 16), F32),
        ),
        in_specs=[vmem] * 4 + [hbm] * 3,
        out_specs=(vmem, vmem),
        scratch_shapes=[
            pltpu.VMEM((8, 96, 256), I32),
            pltpu.VMEM((96, 8, 256), F32),
            pltpu.VMEM((1024, 768), F32),
            pltpu.VMEM((48, 16, 256), BF16),
            pltpu.VMEM((1024, 768), BF16),
            pltpu.VMEM((8, 768, 256), BF16),
            pltpu.VMEM((2, 4, 4, 2, 16, 384), BF16),
            pltpu.VMEM((8, 16, 384), BF16),
            pltpu.VMEM((8, 8, 128), F32),
            pltpu.VMEM((128, 128), I32),
            pltpu.VMEM((16, 1, 128), I32),
            pltpu.VMEM((16, 1, 128), I32),
            pltpu.VMEM((16, 16, 768), BF16),
            pltpu.VMEM((16, 16, 768), BF16),
            pltpu.VMEM((16, 1, 128), F32),
            pltpu.VMEM((16, 1, 128), F32),
            pltpu.VMEM((128, 128), F32),
            pltpu.VMEM((8, 16, 128), F32),
            pltpu.VMEM((16, 128), F32),
            dma((3,)),
            dma((8,)), dma((8,)), dma((8,)), dma((8,)),
            dma((2, 3, 4)), dma((2, 3, 4)),
            dma((16,)), dma((16,)), dma((16,)), dma((16,)),
            dma((16,)), dma((16,)), dma((8,)), dma((8,)),
        ],
        compiler_params=pltpu.CompilerParams(
            vmem_limit_bytes=48 << 20, collective_id=0, has_side_effects=True
        ),
        cost_estimate=pl.CostEstimate(flops=3_000_000_000, bytes_accessed=7_000_000, transcendentals=0),
        name="search",
    )(
        queries,
        probes.T,
        cand_owner,
        cand_row,
        pq_codes,
        codebook.transpose(0, 2, 1),
        vectors,
    )


def solution(mesh):
    both = ("group", "shard")
    in_specs = (
        P(both, None),
        P(),
        P(both, None, None),
        P("group", None),
        P(both, None),
        P(both, None),
        P(both, None),
    )
    out_specs = (P(both, None, None), P(both, None))
    return jax.shard_map(
        per_device, mesh=mesh, in_specs=in_specs, out_specs=out_specs, check_vma=False
    )
```

```python
import jax
import jax.numpy as jnp
from jax import lax
from jax.experimental import pallas as pl
from jax.experimental.pallas import tpu as pltpu
from jax.sharding import PartitionSpec as P

MESH = pl.DeviceIdType.MESH
F32, BF16, I32 = jnp.float32, jnp.bfloat16, jnp.int32


def lane_gather(table, index):
    numbers = lax.GatherDimensionNumbers(
        offset_dims=(),
        collapsed_slice_dims=(1,),
        start_index_map=(1,),
        operand_batching_dims=(0,),
        start_indices_batching_dims=(0,),
    )
    return lax.gather(
        table, index[..., None], numbers, (1, 1), mode=lax.GatherScatterMode.PROMISE_IN_BOUNDS
    )


def iota(shape, dim):
    return lax.broadcasted_iota(I32, shape, dim)


def kernel(
    q_hbm,
    probes_hbm,
    owner_hbm,
    row_hbm,
    codes_hbm,
    book_hbm,
    vectors_hbm,
    pq_ref,
    rr_ref,
    q_ref,
    probes_ref,
    owner_ref,
    row_ref,
    codes,
    book,
    vectors,
    book16,
    vectors16,
    decoded,
    group_q,
    cube_q,
    want_t,
    want_out,
    want_in,
    slot_out,
    slot_in,
    score_out,
    score_in,
    total,
    load_sem,
    cq_s, cq_r,
    g_s, g_r,
    sq_s, sq_r, sw_s, sw_r,
    rs_s, rs_r,
):
    x = lax.axis_index("group")
    s = lax.axis_index("shard")
    y, z, c = s // 8, (s // 2) % 4, s % 2
    me = x * 32 + s
    a = x * 2 + c
    w = y * 4 + z

    def device(x, y, z, c):
        return {"group": x, "shard": (y * 4 + z) * 2 + c}

    def cube_peer(i):
        p = (a + i) % 8
        return p, device(p // 2, y, z, p % 2)

    def plane_peer(i):
        p = (w + i) % 16
        return p, device(x, p // 4, p % 4, c)

    loads = [
        pltpu.make_async_copy(src, dst, load_sem.at[i])
        for i, (src, dst) in enumerate(
            (
                (q_hbm, q_ref),
                (owner_hbm, owner_ref),
                (row_hbm, row_ref),
                (book_hbm, book),
                (codes_hbm, codes),
                (probes_hbm, probes_ref),
                (vectors_hbm, vectors),
            )
        )
    ]
    for load in loads:
        load.start()

    barrier = pltpu.get_barrier_semaphore()
    for i in range(1, 8):
        pl.semaphore_signal(barrier, inc=1, device_id=cube_peer(i)[1], device_id_type=MESH)
    for i in range(1, 16):
        pl.semaphore_signal(barrier, inc=1, device_id=plane_peer(i)[1], device_id_type=MESH)

    def remote(src, dst, send, recv, to):
        return pltpu.make_async_remote_copy(
            src_ref=src, dst_ref=dst, send_sem=send, recv_sem=recv, device_id=to, device_id_type=MESH
        )

    for load in loads[:3]:
        load.wait()
    q = q_ref[...]
    high = q.astype(BF16)
    low = (q - high.astype(F32)).astype(BF16)
    cube_q[a, :, :384] = jnp.concatenate([high[:, :384], high[:, 384:]], axis=0)
    for h in range(2):
        group_q[h, y, z, c] = jnp.concatenate(
            [high[:, h * 384 : h * 384 + 384], low[:, h * 384 : h * 384 + 384]], axis=0
        )
    owner = owner_ref[...]
    row = row_ref[...].astype(F32)
    lanes = iota((8, 128), 1)
    present = jnp.zeros((8, 128), F32)
    wanted = jnp.zeros((8, 128), F32)
    for k in range(16):
        hit = owner[:, k : k + 1] == lanes
        present = jnp.where(hit, 1.0, present)
        wanted = jnp.where(hit, row[:, k : k + 1], wanted)
    earlier = (iota((8, 8), 1) < iota((8, 8), 0)).astype(BF16)
    rank = jnp.dot(earlier, present.astype(BF16), preferred_element_type=F32)
    slot = (a * 2).astype(F32) + rank
    upper = jnp.floor(wanted * (1.0 / 128.0))
    cube_q[a, :, 384:] = jnp.concatenate(
        [jnp.where(present > 0.0, slot * 8.0 + upper, -1.0), wanted - upper * 128.0], axis=0
    ).astype(BF16)

    pl.semaphore_wait(barrier, 22)

    cube_copies = []
    for i in range(1, 8):
        _, to = cube_peer(i)
        copy = remote(cube_q.at[a], cube_q.at[a], cq_s.at[i], cq_r.at[i], to)
        copy.start()
        cube_copies.append(copy)

    def line_peer(axis, i):
        return (
            device(x, (y + i) % 4, z, c) if axis == 0 else device(x, y, (z + i) % 4, c)
        )

    first_copies, second_copies = [], []
    for i in (1, 3, 2):
        for h in range(2):
            block = group_q.at[h, y, z, c]
            copy = remote(block, block, g_s.at[h, 0, i], g_r.at[h, 0, i], line_peer(h, i))
            copy.start()
            first_copies.append(copy)

    loads[3].wait()

    def to_book16(i, _):
        pair = book[pl.ds(i * 2, 2)]
        book16[i] = jnp.concatenate([pair[0], pair[1]], axis=0).astype(BF16)
        return 0

    lax.fori_loop(0, 48, to_book16, 0, unroll=8)
    loads[4].wait()

    def decode(l, _):
        for m in range(48):
            for h in range(2):
                span = slice(h * 128, h * 128 + 128)
                index = jnp.concatenate(
                    [
                        jnp.broadcast_to(codes[l, 2 * m : 2 * m + 1, span], (8, 128)),
                        jnp.broadcast_to(codes[l, 2 * m + 1 : 2 * m + 2, span], (8, 128)),
                    ],
                    axis=0,
                )
                near = (index & 127).astype(jnp.int16)
                decoded[l, m * 16 : m * 16 + 16, span] = jnp.where(
                    index < 128,
                    lane_gather(book16[m, :, :128], near),
                    lane_gather(book16[m, :, 128:], near),
                )
        return 0

    lax.fori_loop(0, 2, decode, 0)

    for copy in cube_copies:
        copy.wait_recv()
    cube = cube_q[...]
    digits = cube[:, :, 384:].astype(F32)
    wants = (digits[:, :8] * 128.0 + digits[:, 8:]).reshape(64, 128)
    wants = jnp.concatenate([wants, jnp.full((64, 128), -1.0, F32)], axis=0)
    want_t[...] = wants.T.astype(I32)
    places = iota((16, 128), 0)
    picks = []
    for p in range(16):
        line = want_t[pl.ds(x * 32 + p * 2 + c, 1), :]
        want_out[p] = line
        picks.append(
            jnp.where((jnp.broadcast_to(line, (16, 128)) >> 10) == places, 1.0, 0.0)
        )
    pick = jnp.concatenate(picks, axis=0)[:, :64].astype(BF16)
    for h in range(2):
        columns = cube[:, h * 8 : h * 8 + 8, :384].reshape(64, 384)
        chosen = jnp.dot(pick, columns, preferred_element_type=F32).astype(BF16)
        slot_out[:, :, h * 384 : h * 384 + 384] = chosen.reshape(16, 16, 384)
    slot_in[w] = slot_out[w]
    want_in[w] = want_out[w]
    slot_copies = []
    for i in range(1, 16):
        p, to = plane_peer(i)
        for copy in (
            remote(slot_out.at[p], slot_in.at[w], sq_s.at[i], sq_r.at[i], to),
            remote(want_out.at[p], want_in.at[w], sw_s.at[i], sw_r.at[i], to),
        ):
            copy.start()
            slot_copies.append(copy)

    for copy in first_copies:
        copy.wait_recv()
    for i in (1, 3, 2):
        for h in range(2):
            block = group_q.at[h, :, z, c] if h == 0 else group_q.at[h, y, :, c]
            copy = remote(block, block, g_s.at[h, 1, i], g_r.at[h, 1, i], line_peer(1 - h, i))
            copy.start()
            second_copies.append(copy)

    lax.fori_loop(2, 5, decode, 0)
    loads[6].wait()

    def to_vectors16(i, _):
        span = pl.ds(pl.multiple_of(i * 128, 128), 128)
        vectors16[span, :] = vectors[span, :].astype(BF16)
        return 0

    lax.fori_loop(0, 8, to_vectors16, 0)

    for copy in second_copies:
        copy.wait_recv()
    sibling = device(x, y, z, 1 - c)
    core_copies = []
    for h in range(2):
        block = group_q.at[h, :, :, c]
        copy = remote(block, block, g_s.at[h, 2, 0], g_r.at[h, 2, 0], sibling)
        copy.start()
        core_copies.append(copy)

    lax.fori_loop(5, 8, decode, 0)

    for copy in slot_copies:
        copy.wait_recv()
    slots = slot_in[...].reshape(256, 768)
    ids = []
    for p in range(16):
        line = jnp.broadcast_to(want_in[p], (16, 128))
        ids.append(jnp.where((line >> 10) == places, line & 1023, 0))
    ids = jnp.sum(jnp.concatenate(ids, axis=0).astype(F32), axis=1, keepdims=True).astype(I32)
    found = jnp.zeros((256, 256), F32)
    for b in range(4):
        part = lax.dot_general(
            slots,
            vectors16[b * 256 : b * 256 + 256, :],
            (((1,), (1,)), ((), ())),
            preferred_element_type=F32,
        )
        found = jnp.where(iota((256, 256), 1) + b * 256 == ids, part, found)
        if b == 0:
            found = jnp.where(iota((256, 256), 1) == ids, part, 0.0)
    scored = jnp.sum(found, axis=1, keepdims=True)
    for p in range(16):
        mine = jnp.broadcast_to(scored[p * 16 : p * 16 + 16, :], (16, 128))
        score_out[p] = jnp.sum(
            jnp.where(iota((16, 128), 1) == places, mine, 0.0), axis=0, keepdims=True
        )
    score_in[me] = score_out[w]
    offsets = [(dx, dy, dz, dc) for dx in range(4) for dy in range(4) for dz in range(4) for dc in range(2)]
    offsets.sort(key=lambda o: -sum(min(d, 4 - d) for d in o[:3]))
    offsets.remove((0, 0, 0, 0))
    for dx, dy, dz, dc in offsets:
        p = (y + dy) % 4 * 4 + (z + dz) % 4
        to = {"group": (x + dx) % 4, "shard": p * 2 + (c + dc) % 2}
        remote(score_out.at[p], score_in.at[me], rs_s.at[0], rs_r.at[0], to).start()

    for copy in core_copies:
        copy.wait_recv()

    loads[5].wait()
    probes = probes_ref[...]

    def score_list(l, _):
        left = jnp.concatenate(
            [group_q[0].reshape(512, 384), group_q[1].reshape(512, 384)], axis=1
        )
        both = jnp.dot(left, decoded[l], preferred_element_type=F32).reshape(32, 2, 8, 256)
        sums = (both[:, 0] + both[:, 1]).reshape(256, 256)
        probed = jnp.max(jnp.where(probes == s * 8 + l, 1.0, 0.0), axis=0, keepdims=True)
        pq_ref[l] = jnp.where(probed > 0.0, sums.T, 0.0)
        return 0

    lax.fori_loop(0, 8, score_list, 0)

    everyone = score_in.at[pl.ds(0, 127)]
    pltpu.make_async_copy(everyone, everyone, rs_r.at[0]).wait()
    total[...] = score_in[...].reshape(128, 128).T
    own = jnp.where(rank < 0.5, total[pl.ds(a * 2, 1), :], total[pl.ds(a * 2 + 1, 1), :])
    result = jnp.zeros((8, 16), F32)
    for k in range(16):
        value = jnp.sum(
            jnp.where(owner[:, k : k + 1] == lanes, own, 0.0), axis=1, keepdims=True
        )
        result = jnp.where(iota((8, 16), 1) == k, value, result)
    rr_ref[...] = result

    for copy in (
        cube_copies + first_copies + second_copies + core_copies + slot_copies
    ):
        copy.wait_send()
    pltpu.make_async_copy(everyone, everyone, rs_s.at[0]).wait()


def hand_over(pq_in, rr_in, pq_ref, rr_ref, pq, rr, sems):
    moves = [(rr_in, rr, rr_ref)] + [(pq_in.at[i], pq.at[i], pq_ref.at[i]) for i in range(8)]
    ins = [pltpu.make_async_copy(a, b, sems.at[0, i]) for i, (a, b, _) in enumerate(moves)]
    outs = [pltpu.make_async_copy(b, c, sems.at[1, i]) for i, (_, b, c) in enumerate(moves)]
    for copy in ins:
        copy.start()
    for copy_in, copy_out in zip(ins, outs):
        copy_in.wait()
        copy_out.start()
    for copy in outs:
        copy.wait()


def per_device(queries, codebook, pq_codes, probes, vectors, cand_owner, cand_row):
    vmem = pl.BlockSpec(memory_space=pltpu.VMEM)
    hbm = pl.BlockSpec(memory_space=pltpu.HBM)
    dma = pltpu.SemaphoreType.DMA
    outs = (
        jax.ShapeDtypeStruct((8, 256, 256), F32),
        jax.ShapeDtypeStruct((8, 16), F32),
    )
    held = pl.pallas_call(
        kernel,
        out_shape=outs,
        in_specs=[hbm] * 7,
        out_specs=(vmem, vmem),
        scratch_shapes=[
            pltpu.VMEM((8, 768), F32),
            pltpu.VMEM((8, 256), I32),
            pltpu.VMEM((8, 16), I32),
            pltpu.VMEM((8, 16), I32),
            pltpu.VMEM((8, 96, 256), I32),
            pltpu.VMEM((96, 8, 256), F32),
            pltpu.VMEM((1024, 768), F32),
            pltpu.VMEM((48, 16, 256), BF16),
            pltpu.VMEM((1024, 768), BF16),
            pltpu.VMEM((8, 768, 256), BF16),
            pltpu.VMEM((2, 4, 4, 2, 16, 384), BF16),
            pltpu.VMEM((8, 16, 512), BF16),
            pltpu.VMEM((128, 128), I32),
            pltpu.VMEM((16, 1, 128), I32),
            pltpu.VMEM((16, 1, 128), I32),
            pltpu.VMEM((16, 16, 768), BF16),
            pltpu.VMEM((16, 16, 768), BF16),
            pltpu.VMEM((16, 1, 128), F32),
            pltpu.VMEM((128, 1, 128), F32),
            pltpu.VMEM((128, 128), F32),
            dma((7,)),
            dma((8,)), dma((8,)),
            dma((2, 3, 4)), dma((2, 3, 4)),
            dma((16,)), dma((16,)), dma((16,)), dma((16,)),
            dma((1,)), dma((1,)),
        ],
        compiler_params=pltpu.CompilerParams(
            vmem_limit_bytes=63 << 20, collective_id=0, has_side_effects=True
        ),
        cost_estimate=pl.CostEstimate(flops=3_000_000_000, bytes_accessed=7_000_000, transcendentals=0),
        name="search",
    )(
        queries,
        probes.T,
        cand_owner,
        cand_row,
        pq_codes,
        codebook.transpose(0, 2, 1),
        vectors,
    )
    return pl.pallas_call(
        hand_over,
        out_shape=outs,
        in_specs=[hbm] * 2,
        out_specs=(hbm, hbm),
        scratch_shapes=[pltpu.VMEM((8, 256, 256), F32), pltpu.VMEM((8, 16), F32), dma((2, 9))],
        compiler_params=pltpu.CompilerParams(vmem_limit_bytes=63 << 20),
        name="hand_over",
    )(*held)


def solution(mesh):
    both = ("group", "shard")
    in_specs = (
        P(both, None),
        P(),
        P(both, None, None),
        P("group", None),
        P(both, None),
        P(both, None),
        P(both, None),
    )
    out_specs = (P(both, None, None), P(both, None))
    return jax.shard_map(
        per_device, mesh=mesh, in_specs=in_specs, out_specs=out_specs, check_vma=False
    )
```

```python
import jax
import jax.numpy as jnp
from jax import lax
from jax.experimental import pallas as pl
from jax.experimental.pallas import tpu as pltpu
from jax.sharding import PartitionSpec as P

MESH = pl.DeviceIdType.MESH
F32, BF16, I32 = jnp.float32, jnp.bfloat16, jnp.int32


def lane_gather(table, index):
    numbers = lax.GatherDimensionNumbers(
        offset_dims=(),
        collapsed_slice_dims=(1,),
        start_index_map=(1,),
        operand_batching_dims=(0,),
        start_indices_batching_dims=(0,),
    )
    return lax.gather(
        table, index[..., None], numbers, (1, 1), mode=lax.GatherScatterMode.PROMISE_IN_BOUNDS
    )


def iota(shape, dim):
    return lax.broadcasted_iota(I32, shape, dim)


def kernel(
    q_hbm,
    probes_hbm,
    owner_hbm,
    row_hbm,
    codes_hbm,
    book_hbm,
    vectors_hbm,
    pq_ref,
    rr_ref,
    q_ref,
    probes_ref,
    owner_ref,
    row_ref,
    codes,
    book,
    vectors,
    book16,
    vectors16,
    decoded,
    group_q,
    cube_q,
    want_t,
    want_out,
    want_in,
    slot_out,
    slot_in,
    score_out,
    score_in,
    total,
    load_sem,
    plane_sem,
    cq_s, cq_r,
    g_s, g_r,
    sq_s, sq_r, sw_s, sw_r,
    rs_s, rs_r,
):
    x = lax.axis_index("group")
    s = lax.axis_index("shard")
    y, z, c = s // 8, (s // 2) % 4, s % 2
    me = x * 32 + s
    a = x * 2 + c
    w = y * 4 + z

    def device(x, y, z, c):
        return {"group": x, "shard": (y * 4 + z) * 2 + c}

    def cube_peer(i):
        p = (a + i) % 8
        return p, device(p // 2, y, z, p % 2)

    def plane_peer(i):
        p = (w + i) % 16
        return p, device(x, p // 4, p % 4, c)

    def line_peer(axis, i):
        return (
            device(x, (y + i) % 4, z, c) if axis == 0 else device(x, y, (z + i) % 4, c)
        )

    barrier = pltpu.get_barrier_semaphore()
    for i in (2, 1, 3):
        for axis in range(2):
            pl.semaphore_signal(barrier, inc=1, device_id=line_peer(axis, i), device_id_type=MESH)
    for i in (4, 5, 2, 3, 6, 7, 1):
        pl.semaphore_signal(barrier, inc=1, device_id=cube_peer(i)[1], device_id_type=MESH)

    loads = [
        pltpu.make_async_copy(src, dst, load_sem.at[i])
        for i, (src, dst) in enumerate(
            (
                (q_hbm, q_ref),
                (owner_hbm, owner_ref),
                (row_hbm, row_ref),
                (book_hbm, book),
                (codes_hbm, codes),
                (probes_hbm, probes_ref),
                (vectors_hbm, vectors),
            )
        )
    ]
    for load in loads:
        load.start()

    def remote(src, dst, send, recv, to):
        return pltpu.make_async_remote_copy(
            src_ref=src, dst_ref=dst, send_sem=send, recv_sem=recv, device_id=to, device_id_type=MESH
        )

    for load in loads[:3]:
        load.wait()
    q = q_ref[...]
    high = q.astype(BF16)
    low = (q - high.astype(F32)).astype(BF16)
    cube_q[a, :, :384] = jnp.concatenate([high[:, :384], high[:, 384:]], axis=0)
    for h in range(2):
        group_q[h, y, z, c] = jnp.concatenate(
            [high[:, h * 384 : h * 384 + 384], low[:, h * 384 : h * 384 + 384]], axis=0
        )
    owner = owner_ref[...]
    row = row_ref[...].astype(F32)
    lanes = iota((8, 128), 1)
    present = jnp.zeros((8, 128), F32)
    wanted = jnp.zeros((8, 128), F32)
    for k in range(16):
        hit = owner[:, k : k + 1] == lanes
        present = jnp.where(hit, 1.0, present)
        wanted = jnp.where(hit, row[:, k : k + 1], wanted)
    earlier = (iota((8, 8), 1) < iota((8, 8), 0)).astype(BF16)
    rank = jnp.dot(earlier, present.astype(BF16), preferred_element_type=F32)
    slot = (a * 2).astype(F32) + rank
    upper = jnp.floor(wanted * (1.0 / 128.0))
    cube_q[a, :, 384:] = jnp.concatenate(
        [jnp.where(present > 0.0, slot * 8.0 + upper, -1.0), wanted - upper * 128.0], axis=0
    ).astype(BF16)

    pl.semaphore_wait(barrier, 13)

    cube_copies = []
    for i in range(1, 8):
        _, to = cube_peer(i)
        copy = remote(cube_q.at[a], cube_q.at[a], cq_s.at[i], cq_r.at[i], to)
        copy.start()
        cube_copies.append(copy)

    for i in (2, 1, 3):
        pl.semaphore_signal(plane_sem, inc=1, device_id=line_peer(1, i), device_id_type=MESH)

    first_copies, second_copies = [], []
    for i in (1, 3, 2):
        for h in range(2):
            block = group_q.at[h, y, z, c]
            copy = remote(block, block, g_s.at[h, 0, i], g_r.at[h, 0, i], line_peer(h, i))
            copy.start()
            first_copies.append(copy)

    loads[3].wait()

    def to_book16(i, _):
        pair = book[pl.ds(i * 2, 2)]
        book16[i] = jnp.concatenate([pair[0], pair[1]], axis=0).astype(BF16)
        return 0

    lax.fori_loop(0, 48, to_book16, 0, unroll=8)
    loads[4].wait()

    def decode(l, _):
        for m in range(48):
            for h in range(2):
                span = slice(h * 128, h * 128 + 128)
                index = jnp.concatenate(
                    [
                        jnp.broadcast_to(codes[l, 2 * m : 2 * m + 1, span], (8, 128)),
                        jnp.broadcast_to(codes[l, 2 * m + 1 : 2 * m + 2, span], (8, 128)),
                    ],
                    axis=0,
                )
                near = (index & 127).astype(jnp.int16)
                decoded[l, m * 16 : m * 16 + 16, span] = jnp.where(
                    index < 128,
                    lane_gather(book16[m, :, :128], near),
                    lane_gather(book16[m, :, 128:], near),
                )
        return 0

    lax.fori_loop(0, 6, decode, 0)

    for copy in cube_copies:
        copy.wait_recv()
    for copy in first_copies:
        copy.wait_recv()
    for i in (1, 3, 2):
        for h in range(2):
            block = group_q.at[h, :, z, c] if h == 0 else group_q.at[h, y, :, c]
            copy = remote(block, block, g_s.at[h, 1, i], g_r.at[h, 1, i], line_peer(1 - h, i))
            copy.start()
            second_copies.append(copy)
    pl.semaphore_wait(plane_sem, 3)
    cube = cube_q[...]
    digits = cube[:, :, 384:].astype(F32)
    wants = (digits[:, :8] * 128.0 + digits[:, 8:]).reshape(64, 128)
    wants = jnp.concatenate([wants, jnp.full((64, 128), -1.0, F32)], axis=0)
    want_t[...] = wants.T.astype(I32)
    places = iota((16, 128), 0)
    picks = []
    for p in range(16):
        line = want_t[pl.ds(x * 32 + p * 2 + c, 1), :]
        want_out[p] = line
        picks.append(
            jnp.where((jnp.broadcast_to(line, (16, 128)) >> 10) == places, 1.0, 0.0)
        )
    pick = jnp.concatenate(picks, axis=0)[:, :64].astype(BF16)
    for h in range(2):
        columns = cube[:, h * 8 : h * 8 + 8, :384].reshape(64, 384)
        chosen = jnp.dot(pick, columns, preferred_element_type=F32).astype(BF16)
        slot_out[:, :, h * 384 : h * 384 + 384] = chosen.reshape(16, 16, 384)
    slot_in[w] = slot_out[w]
    want_in[w] = want_out[w]
    slot_copies = []
    for i in range(1, 16):
        p, to = plane_peer(i)
        for copy in (
            remote(slot_out.at[p], slot_in.at[w], sq_s.at[i], sq_r.at[i], to),
            remote(want_out.at[p], want_in.at[w], sw_s.at[i], sw_r.at[i], to),
        ):
            copy.start()
            slot_copies.append(copy)

    lax.fori_loop(6, 8, decode, 0)
    loads[6].wait()

    def to_vectors16(i, _):
        span = pl.ds(pl.multiple_of(i * 128, 128), 128)
        vectors16[span, :] = vectors[span, :].astype(BF16)
        return 0

    lax.fori_loop(0, 8, to_vectors16, 0)

    for copy in second_copies:
        copy.wait_recv()
    sibling = device(x, y, z, 1 - c)
    core_copies = []
    for h in range(2):
        block = group_q.at[h, :, :, c]
        copy = remote(block, block, g_s.at[h, 2, 0], g_r.at[h, 2, 0], sibling)
        copy.start()
        core_copies.append(copy)

    for copy in slot_copies:
        copy.wait_recv()
    slots = slot_in[...].reshape(256, 768)
    ids = []
    for p in range(16):
        line = jnp.broadcast_to(want_in[p], (16, 128))
        ids.append(jnp.where((line >> 10) == places, line & 1023, 0))
    ids = jnp.sum(jnp.concatenate(ids, axis=0).astype(F32), axis=1, keepdims=True).astype(I32)
    found = jnp.zeros((256, 256), F32)
    for b in range(4):
        part = lax.dot_general(
            slots,
            vectors16[b * 256 : b * 256 + 256, :],
            (((1,), (1,)), ((), ())),
            preferred_element_type=F32,
        )
        found = jnp.where(iota((256, 256), 1) + b * 256 == ids, part, found)
        if b == 0:
            found = jnp.where(iota((256, 256), 1) == ids, part, 0.0)
    scored = jnp.sum(found, axis=1, keepdims=True)
    for p in range(16):
        mine = jnp.broadcast_to(scored[p * 16 : p * 16 + 16, :], (16, 128))
        score_out[p] = jnp.sum(
            jnp.where(iota((16, 128), 1) == places, mine, 0.0), axis=0, keepdims=True
        )
    score_in[me] = score_out[w]
    offsets = [(dx, dy, dz, dc) for dx in range(4) for dy in range(4) for dz in range(4) for dc in range(2)]
    offsets.sort(key=lambda o: -sum(min(d, 4 - d) for d in o[:3]))
    offsets.remove((0, 0, 0, 0))
    for dx, dy, dz, dc in offsets:
        p = (y + dy) % 4 * 4 + (z + dz) % 4
        to = {"group": (x + dx) % 4, "shard": p * 2 + (c + dc) % 2}
        remote(score_out.at[p], score_in.at[me], rs_s.at[0], rs_r.at[0], to).start()

    for copy in core_copies:
        copy.wait_recv()

    loads[5].wait()
    probes = probes_ref[...]

    def score_list(l, _):
        left = jnp.concatenate(
            [group_q[0].reshape(512, 384), group_q[1].reshape(512, 384)], axis=1
        )
        both = jnp.dot(left, decoded[l], preferred_element_type=F32).reshape(32, 2, 8, 256)
        sums = (both[:, 0] + both[:, 1]).reshape(256, 256)
        probed = jnp.max(jnp.where(probes == s * 8 + l, 1.0, 0.0), axis=0, keepdims=True)
        pq_ref[l] = jnp.where(probed > 0.0, sums.T, 0.0)
        return 0

    lax.fori_loop(0, 8, score_list, 0)

    everyone = score_in.at[pl.ds(0, 127)]
    pltpu.make_async_copy(everyone, everyone, rs_r.at[0]).wait()
    total[...] = score_in[...].reshape(128, 128).T
    own = jnp.where(rank < 0.5, total[pl.ds(a * 2, 1), :], total[pl.ds(a * 2 + 1, 1), :])
    result = jnp.zeros((8, 16), F32)
    for k in range(16):
        value = jnp.sum(
            jnp.where(owner[:, k : k + 1] == lanes, own, 0.0), axis=1, keepdims=True
        )
        result = jnp.where(iota((8, 16), 1) == k, value, result)
    rr_ref[...] = result

    for copy in (
        cube_copies + first_copies + second_copies + core_copies + slot_copies
    ):
        copy.wait_send()
    pltpu.make_async_copy(everyone, everyone, rs_s.at[0]).wait()


def hand_over(pq_in, rr_in, pq_ref, rr_ref, sems):
    copies = [pltpu.make_async_copy(rr_in, rr_ref, sems.at[8])]
    copies += [pltpu.make_async_copy(pq_in.at[i], pq_ref.at[i], sems.at[i]) for i in range(8)]
    for copy in copies:
        copy.start()
    for copy in copies:
        copy.wait()


def per_device(queries, codebook, pq_codes, probes, vectors, cand_owner, cand_row):
    vmem = pl.BlockSpec(memory_space=pltpu.VMEM)
    hbm = pl.BlockSpec(memory_space=pltpu.HBM)
    dma = pltpu.SemaphoreType.DMA
    outs = (
        jax.ShapeDtypeStruct((8, 256, 256), F32),
        jax.ShapeDtypeStruct((8, 16), F32),
    )
    held = pl.pallas_call(
        kernel,
        out_shape=outs,
        in_specs=[hbm] * 7,
        out_specs=(vmem, vmem),
        scratch_shapes=[
            pltpu.VMEM((8, 768), F32),
            pltpu.VMEM((8, 256), I32),
            pltpu.VMEM((8, 16), I32),
            pltpu.VMEM((8, 16), I32),
            pltpu.VMEM((8, 96, 256), I32),
            pltpu.VMEM((96, 8, 256), F32),
            pltpu.VMEM((1024, 768), F32),
            pltpu.VMEM((48, 16, 256), BF16),
            pltpu.VMEM((1024, 768), BF16),
            pltpu.VMEM((8, 768, 256), BF16),
            pltpu.VMEM((2, 4, 4, 2, 16, 384), BF16),
            pltpu.VMEM((8, 16, 512), BF16),
            pltpu.VMEM((128, 128), I32),
            pltpu.VMEM((16, 1, 128), I32),
            pltpu.VMEM((16, 1, 128), I32),
            pltpu.VMEM((16, 16, 768), BF16),
            pltpu.VMEM((16, 16, 768), BF16),
            pltpu.VMEM((16, 1, 128), F32),
            pltpu.VMEM((128, 1, 128), F32),
            pltpu.VMEM((128, 128), F32),
            dma((7,)),
            pltpu.SemaphoreType.REGULAR,
            dma((8,)), dma((8,)),
            dma((2, 3, 4)), dma((2, 3, 4)),
            dma((16,)), dma((16,)), dma((16,)), dma((16,)),
            dma((1,)), dma((1,)),
        ],
        compiler_params=pltpu.CompilerParams(
            vmem_limit_bytes=32 << 20, collective_id=0, has_side_effects=True
        ),
        cost_estimate=pl.CostEstimate(flops=3_000_000_000, bytes_accessed=7_000_000, transcendentals=0),
        name="search",
    )(
        *(
            pltpu.with_memory_space_constraint(operand, pltpu.HBM)
            for operand in (
                queries,
                probes.T,
                cand_owner,
                cand_row,
                pq_codes,
                codebook.transpose(0, 2, 1),
                vectors,
            )
        )
    )
    return pl.pallas_call(
        hand_over,
        out_shape=outs,
        in_specs=[pl.BlockSpec(memory_space=pl.ANY)] * 2,
        out_specs=(hbm, hbm),
        scratch_shapes=[dma((9,))],
        compiler_params=pltpu.CompilerParams(vmem_limit_bytes=16 << 20),
        name="hand_over",
    )(*held)


def solution(mesh):
    both = ("group", "shard")
    in_specs = (
        P(both, None),
        P(),
        P(both, None, None),
        P("group", None),
        P(both, None),
        P(both, None),
        P(both, None),
    )
    out_specs = (P(both, None, None), P(both, None))
    return jax.shard_map(
        per_device, mesh=mesh, in_specs=in_specs, out_specs=out_specs, check_vma=False
    )
```

```python
import jax
import jax.numpy as jnp
from jax import lax
from jax.experimental import pallas as pl
from jax.experimental.pallas import tpu as pltpu
from jax.sharding import PartitionSpec as P

MESH = pl.DeviceIdType.MESH
F32, BF16, I32 = jnp.float32, jnp.bfloat16, jnp.int32
GROUP = 16


def lane_gather(table, index):
    numbers = lax.GatherDimensionNumbers(
        offset_dims=(),
        collapsed_slice_dims=(1,),
        start_index_map=(1,),
        operand_batching_dims=(0,),
        start_indices_batching_dims=(0,),
    )
    return lax.gather(
        table, index[..., None], numbers, (1, 1), mode=lax.GatherScatterMode.PROMISE_IN_BOUNDS
    )


def iota(shape, dim):
    return lax.broadcasted_iota(I32, shape, dim)


def kernel(
    q_hbm,
    probes_hbm,
    owner_hbm,
    row_hbm,
    codes_hbm,
    book_hbm,
    vectors_hbm,
    pq_ref,
    rr_ref,
    q_ref,
    probes_ref,
    owner_ref,
    row_ref,
    codes,
    book,
    vectors,
    book16,
    vectors16,
    decoded,
    group_q,
    cube_q,
    slot_t,
    place_t,
    row_t,
    want_out,
    want_in,
    slot_out,
    slot_in,
    score_out,
    score_in,
    total,
    load_sem,
    plane_sem,
    cq_s, cq_r,
    g_s, g_r,
    sq_s, sq_r, sw_s, sw_r,
    rs_s, rs_r,
):
    x = lax.axis_index("group")
    s = lax.axis_index("shard")
    y, z, c = s // 8, (s // 2) % 4, s % 2
    me = x * 32 + s
    a = x * 2 + c
    w = y * 4 + z

    def device(x, y, z, c):
        return {"group": x, "shard": (y * 4 + z) * 2 + c}

    def cube_peer(i):
        p = (a + i) % 8
        return p, device(p // 2, y, z, p % 2)

    def plane_peer(dy, dz):
        to_y, to_z = (y + dy) % 4, (z + dz) % 4
        return to_y * 4 + to_z, device(x, to_y, to_z, c)

    plane_offsets = [(dy, dz) for dy in range(4) for dz in range(4)]
    plane_offsets.sort(key=lambda o: -sum(min(d, 4 - d) for d in o))

    def line_peer(axis, i):
        return (
            device(x, (y + i) % 4, z, c) if axis == 0 else device(x, y, (z + i) % 4, c)
        )

    barrier = pltpu.get_barrier_semaphore()
    for i in (2, 1, 3):
        for axis in range(2):
            pl.semaphore_signal(barrier, inc=1, device_id=line_peer(axis, i), device_id_type=MESH)
    for i in (4, 5, 2, 3, 6, 7, 1):
        pl.semaphore_signal(barrier, inc=1, device_id=cube_peer(i)[1], device_id_type=MESH)

    loads = [
        pltpu.make_async_copy(src, dst, load_sem.at[i])
        for i, (src, dst) in enumerate(
            (
                (q_hbm, q_ref),
                (owner_hbm, owner_ref),
                (row_hbm, row_ref),
                (book_hbm, book),
                (codes_hbm, codes),
                (probes_hbm, probes_ref),
                (vectors_hbm, vectors),
            )
        )
    ]
    for load in loads:
        load.start()

    def remote(src, dst, send, recv, to):
        return pltpu.make_async_remote_copy(
            src_ref=src, dst_ref=dst, send_sem=send, recv_sem=recv, device_id=to, device_id_type=MESH
        )

    for load in loads[:3]:
        load.wait()
    q = q_ref[...]
    high = q.astype(BF16)
    low = (q - high.astype(F32)).astype(BF16)
    cube_q[a, :, :384] = jnp.concatenate([high[:, :384], high[:, 384:]], axis=0)
    for h in range(2):
        group_q[h, y, z, c] = jnp.concatenate(
            [high[:, h * 384 : h * 384 + 384], low[:, h * 384 : h * 384 + 384]], axis=0
        )
    owner = owner_ref[...]
    row = row_ref[...].astype(F32)
    lanes = iota((8, 128), 1)
    present = jnp.zeros((8, 128), F32)
    wanted = jnp.zeros((8, 128), F32)
    for k in range(16):
        hit = owner[:, k : k + 1] == lanes
        present = jnp.where(hit, 1.0, present)
        wanted = jnp.where(hit, row[:, k : k + 1], wanted)
    earlier = (iota((8, 8), 1) < iota((8, 8), 0)).astype(BF16)
    rank = jnp.dot(earlier, present.astype(BF16), preferred_element_type=F32)
    slot = (a * 2).astype(F32) + rank
    rows = [
        jnp.sum(jnp.where((present > 0.0) & (rank == float(k)), wanted, 0.0), axis=0, keepdims=True)
        for k in range(2)
    ]
    rows = jnp.concatenate(rows + [jnp.zeros((6, 128), F32)], axis=0)
    upper = jnp.floor(rows * (1.0 / 32.0))
    digits = upper + pltpu.roll(rows - upper * 32.0, 2, 0)
    cube_q[a, :, 384:] = jnp.concatenate(
        [jnp.where(present > 0.0, slot, -1.0), digits], axis=0
    ).astype(BF16)
    place_t[...] = jnp.zeros((128, 128), F32)

    pl.semaphore_wait(barrier, 13)

    cube_copies = []
    for i in range(1, 8):
        _, to = cube_peer(i)
        copy = remote(cube_q.at[a], cube_q.at[a], cq_s.at[i], cq_r.at[i], to)
        copy.start()
        cube_copies.append(copy)

    for i in (2, 1, 3):
        pl.semaphore_signal(plane_sem, inc=1, device_id=line_peer(1, i), device_id_type=MESH)

    first_copies, second_copies = [], []
    for i in (1, 3, 2):
        for h in range(2):
            block = group_q.at[h, y, z, c]
            copy = remote(block, block, g_s.at[h, 0, i], g_r.at[h, 0, i], line_peer(h, i))
            copy.start()
            first_copies.append(copy)

    loads[3].wait()

    def to_book16(i, _):
        pair = book[pl.ds(i * 2, 2)]
        book16[i] = jnp.concatenate([pair[0], pair[1]], axis=0).astype(BF16)
        return 0

    lax.fori_loop(0, 48, to_book16, 0, unroll=8)
    loads[4].wait()

    def decode(l, _):
        for m in range(48):
            for h in range(2):
                span = slice(h * 128, h * 128 + 128)
                index = jnp.concatenate(
                    [
                        jnp.broadcast_to(codes[l, 2 * m : 2 * m + 1, span], (8, 128)),
                        jnp.broadcast_to(codes[l, 2 * m + 1 : 2 * m + 2, span], (8, 128)),
                    ],
                    axis=0,
                )
                near = (index & 127).astype(jnp.int16)
                decoded[l, m * 16 : m * 16 + 16, span] = jnp.where(
                    index < 128,
                    lane_gather(book16[m, :, :128], near),
                    lane_gather(book16[m, :, 128:], near),
                )
        return 0

    lax.fori_loop(0, 6, decode, 0)

    for copy in cube_copies:
        copy.wait_recv()
    pl.semaphore_wait(plane_sem, 3)
    cube = cube_q[...]
    codes_in = cube[:, :, 384:].astype(F32)
    slot_t[...] = jnp.concatenate(
        [codes_in[:, :8].reshape(64, 128), jnp.full((64, 128), -1.0, F32)], axis=0
    ).T
    for k in range(8):
        pair = codes_in[k, 8:10] * 32.0 + codes_in[k, 10:12]
        place_t[pl.ds(pl.multiple_of(w % 8 * 16, 16), 16), :] += jnp.pad(
            pair, ((2 * k, 14 - 2 * k), (0, 0))
        )
    row_t[...] = place_t[...].T
    columns = [cube[:, h * 8 : h * 8 + 8, :384].reshape(64, 384) for h in range(2)]
    columns = jnp.concatenate(columns, axis=1)
    places = iota((16, 128), 0).astype(F32)
    slot_copies = []
    for first in range(0, 16, GROUP):
        group = plane_offsets[first : first + GROUP]
        picks = []
        for dy, dz in group:
            p, _ = plane_peer(dy, dz)
            line = pl.ds(x * 32 + p * 2 + c, 1)
            want_out[dy * 4 + dz] = row_t[line, :]
            picks.append(
                jnp.where(jnp.broadcast_to(slot_t[line, :], (16, 128)) == places, 1.0, 0.0)
            )
        pick = jnp.concatenate(picks, axis=0)[:, :64].astype(BF16)
        chosen = jnp.dot(pick, columns, preferred_element_type=F32).astype(BF16)
        for n, (dy, dz) in enumerate(group):
            k = dy * 4 + dz
            if k == 0:
                slot_in[w] = chosen[n * 16 : n * 16 + 16]
                want_in[w] = want_out[0]
                continue
            slot_out[k] = chosen[n * 16 : n * 16 + 16]
            _, to = plane_peer(dy, dz)
            for copy in (
                remote(want_out.at[k], want_in.at[w], sw_s.at[k], sw_r.at[k], to),
                remote(slot_out.at[k], slot_in.at[w], sq_s.at[k], sq_r.at[k], to),
            ):
                copy.start()
                slot_copies.append(copy)

    lax.fori_loop(6, 8, decode, 0)
    for copy in first_copies:
        copy.wait_recv()
    for i in (1, 3, 2):
        for h in range(2):
            block = group_q.at[h, :, z, c] if h == 0 else group_q.at[h, y, :, c]
            copy = remote(block, block, g_s.at[h, 1, i], g_r.at[h, 1, i], line_peer(1 - h, i))
            copy.start()
            second_copies.append(copy)
    loads[6].wait()

    def to_vectors16(i, _):
        span = pl.ds(pl.multiple_of(i * 128, 128), 128)
        vectors16[span, :] = vectors[span, :].astype(BF16)
        return 0

    lax.fori_loop(0, 8, to_vectors16, 0)

    for copy in slot_copies:
        copy.wait_recv()
    slots = slot_in[...].reshape(256, 768)
    ids = jnp.concatenate(
        [jnp.sum(want_in[b * 8 : b * 8 + 8], axis=0) for b in range(2)], axis=1
    ).astype(I32)
    found = jnp.zeros((256, 256), F32)
    for b in range(4):
        part = lax.dot_general(
            vectors16[b * 256 : b * 256 + 256, :],
            slots,
            (((1,), (1,)), ((), ())),
            preferred_element_type=F32,
        )
        found = jnp.where(iota((256, 256), 0) + b * 256 == ids, part, found)
    scored = jnp.sum(found, axis=0, keepdims=True)
    for b in range(2):
        score_out[b] = scored[:, b * 128 : b * 128 + 128]
    score_in[me] = score_out[w // 8]
    offsets = [(dx, dy, dz, dc) for dx in range(4) for dy in range(4) for dz in range(4) for dc in range(2)]
    offsets.sort(key=lambda o: -sum(min(d, 4 - d) for d in o[:3]))
    offsets.remove((0, 0, 0, 0))
    for dx, dy, dz, dc in offsets:
        p = (y + dy) % 4 * 4 + (z + dz) % 4
        to = {"group": (x + dx) % 4, "shard": p * 2 + (c + dc) % 2}
        remote(score_out.at[p // 8], score_in.at[me], rs_s.at[0], rs_r.at[0], to).start()

    for copy in second_copies:
        copy.wait_recv()
    sibling = device(x, y, z, 1 - c)
    core_copies = []
    for h in range(2):
        block = group_q.at[h, :, :, c]
        copy = remote(block, block, g_s.at[h, 2, 0], g_r.at[h, 2, 0], sibling)
        copy.start()
        core_copies.append(copy)
    for copy in core_copies:
        copy.wait_recv()

    loads[5].wait()
    probes = probes_ref[...]

    def score_list(l, _):
        left = jnp.concatenate(
            [group_q[0].reshape(512, 384), group_q[1].reshape(512, 384)], axis=1
        )
        both = jnp.dot(left, decoded[l], preferred_element_type=F32).reshape(32, 2, 8, 256)
        sums = (both[:, 0] + both[:, 1]).reshape(256, 256)
        probed = jnp.max(jnp.where(probes == s * 8 + l, 1.0, 0.0), axis=0, keepdims=True)
        pq_ref[l] = jnp.where(probed > 0.0, sums.T, 0.0)
        return 0

    lax.fori_loop(0, 8, score_list, 0)

    everyone = score_in.at[pl.ds(0, 127)]
    pltpu.make_async_copy(everyone, everyone, rs_r.at[0]).wait()
    total[...] = score_in[...].reshape(128, 128).T
    line = w % 8 * 16 + a * 2
    own = jnp.where(rank < 0.5, total[pl.ds(line, 1), :], total[pl.ds(line + 1, 1), :])
    result = jnp.zeros((8, 16), F32)
    for k in range(16):
        value = jnp.sum(
            jnp.where(owner[:, k : k + 1] == lanes, own, 0.0), axis=1, keepdims=True
        )
        result = jnp.where(iota((8, 16), 1) == k, value, result)
    rr_ref[...] = result

    for copy in (
        cube_copies + first_copies + second_copies + core_copies + slot_copies
    ):
        copy.wait_send()
    pltpu.make_async_copy(everyone, everyone, rs_s.at[0]).wait()


def hand_over(pq_in, rr_in, pq_ref, rr_ref, sems):
    copies = [pltpu.make_async_copy(rr_in, rr_ref, sems.at[8])]
    copies += [pltpu.make_async_copy(pq_in.at[i], pq_ref.at[i], sems.at[i]) for i in range(8)]
    for copy in copies:
        copy.start()
    for copy in copies:
        copy.wait()


def per_device(queries, codebook, pq_codes, probes, vectors, cand_owner, cand_row):
    vmem = pl.BlockSpec(memory_space=pltpu.VMEM)
    hbm = pl.BlockSpec(memory_space=pltpu.HBM)
    dma = pltpu.SemaphoreType.DMA
    outs = (
        jax.ShapeDtypeStruct((8, 256, 256), F32),
        jax.ShapeDtypeStruct((8, 16), F32),
    )
    held = pl.pallas_call(
        kernel,
        out_shape=outs,
        in_specs=[hbm] * 7,
        out_specs=(vmem, vmem),
        scratch_shapes=[
            pltpu.VMEM((8, 768), F32),
            pltpu.VMEM((8, 256), I32),
            pltpu.VMEM((8, 16), I32),
            pltpu.VMEM((8, 16), I32),
            pltpu.VMEM((8, 96, 256), I32),
            pltpu.VMEM((96, 8, 256), F32),
            pltpu.VMEM((1024, 768), F32),
            pltpu.VMEM((48, 16, 256), BF16),
            pltpu.VMEM((1024, 768), BF16),
            pltpu.VMEM((8, 768, 256), BF16),
            pltpu.VMEM((2, 4, 4, 2, 16, 384), BF16),
            pltpu.VMEM((8, 16, 512), BF16),
            pltpu.VMEM((128, 128), F32),
            pltpu.VMEM((128, 128), F32),
            pltpu.VMEM((128, 128), F32),
            pltpu.VMEM((16, 1, 128), F32),
            pltpu.VMEM((16, 1, 128), F32),
            pltpu.VMEM((16, 16, 768), BF16),
            pltpu.VMEM((16, 16, 768), BF16),
            pltpu.VMEM((2, 1, 128), F32),
            pltpu.VMEM((128, 1, 128), F32),
            pltpu.VMEM((128, 128), F32),
            dma((7,)),
            pltpu.SemaphoreType.REGULAR,
            dma((8,)), dma((8,)),
            dma((2, 3, 4)), dma((2, 3, 4)),
            dma((16,)), dma((16,)), dma((16,)), dma((16,)),
            dma((1,)), dma((1,)),
        ],
        compiler_params=pltpu.CompilerParams(
            vmem_limit_bytes=32 << 20, collective_id=0, has_side_effects=True
        ),
        cost_estimate=pl.CostEstimate(flops=3_000_000_000, bytes_accessed=7_000_000, transcendentals=0),
        name="search",
    )(
        *(
            pltpu.with_memory_space_constraint(operand, pltpu.HBM)
            for operand in (
                queries,
                probes.T,
                cand_owner,
                cand_row,
                pq_codes,
                codebook.transpose(0, 2, 1),
                vectors,
            )
        )
    )
    return pl.pallas_call(
        hand_over,
        out_shape=outs,
        in_specs=[pl.BlockSpec(memory_space=pl.ANY)] * 2,
        out_specs=(hbm, hbm),
        scratch_shapes=[dma((9,))],
        compiler_params=pltpu.CompilerParams(vmem_limit_bytes=16 << 20),
        name="hand_over",
    )(*held)


def solution(mesh):
    both = ("group", "shard")
    in_specs = (
        P(both, None),
        P(),
        P(both, None, None),
        P("group", None),
        P(both, None),
        P(both, None),
        P(both, None),
    )
    out_specs = (P(both, None, None), P(both, None))
    return jax.shard_map(
        per_device, mesh=mesh, in_specs=in_specs, out_specs=out_specs, check_vma=False
    )
```

```python
import jax
import jax.numpy as jnp
from jax import lax
from jax.experimental import pallas as pl
from jax.experimental.pallas import tpu as pltpu
from jax.sharding import PartitionSpec as P

MESH = pl.DeviceIdType.MESH
F32, BF16, I32 = jnp.float32, jnp.bfloat16, jnp.int32
GROUP = 16


def lane_gather(table, index):
    numbers = lax.GatherDimensionNumbers(
        offset_dims=(),
        collapsed_slice_dims=(1,),
        start_index_map=(1,),
        operand_batching_dims=(0,),
        start_indices_batching_dims=(0,),
    )
    return lax.gather(
        table, index[..., None], numbers, (1, 1), mode=lax.GatherScatterMode.PROMISE_IN_BOUNDS
    )


def iota(shape, dim):
    return lax.broadcasted_iota(I32, shape, dim)


def kernel(
    q_hbm,
    probes_hbm,
    owner_hbm,
    row_hbm,
    codes_hbm,
    book_hbm,
    vectors_hbm,
    pq_ref,
    rr_ref,
    q_ref,
    probes_ref,
    owner_ref,
    row_ref,
    codes,
    book,
    vectors,
    book16,
    vectors16,
    decoded,
    group_q,
    cube_q,
    slot_t,
    place_t,
    row_t,
    want_out,
    want_in,
    slot_out,
    slot_in,
    score_out,
    score_in,
    total,
    load_sem,
    plane_sem,
    cq_s, cq_r,
    g_s, g_r,
    sq_s, sq_r, sw_s, sw_r,
    rs_s, rs_r,
):
    x = lax.axis_index("group")
    s = lax.axis_index("shard")
    y, z, c = s // 8, (s // 2) % 4, s % 2
    me = x * 32 + s
    a = x * 2 + c
    w = y * 4 + z

    def device(x, y, z, c):
        return {"group": x, "shard": (y * 4 + z) * 2 + c}

    def cube_peer(i):
        p = (a + i) % 8
        return p, device(p // 2, y, z, p % 2)

    def plane_peer(dy, dz):
        to_y, to_z = (y + dy) % 4, (z + dz) % 4
        return to_y * 4 + to_z, device(x, to_y, to_z, c)

    plane_offsets = [(dy, dz) for dy in range(4) for dz in range(4)]
    plane_offsets.sort(key=lambda o: -sum(min(d, 4 - d) for d in o))

    def line_peer(axis, i):
        return (
            device(x, (y + i) % 4, z, c) if axis == 0 else device(x, y, (z + i) % 4, c)
        )

    barrier = pltpu.get_barrier_semaphore()
    for i in (2, 1, 3):
        for axis in range(2):
            pl.semaphore_signal(barrier, inc=1, device_id=line_peer(axis, i), device_id_type=MESH)
    for i in (4, 5, 2, 3, 6, 7, 1):
        pl.semaphore_signal(barrier, inc=1, device_id=cube_peer(i)[1], device_id_type=MESH)

    loads = [
        pltpu.make_async_copy(src, dst, load_sem.at[i])
        for i, (src, dst) in enumerate(
            (
                (q_hbm, q_ref),
                (owner_hbm, owner_ref),
                (row_hbm, row_ref),
                (book_hbm, book),
                (codes_hbm, codes),
                (probes_hbm, probes_ref),
                (vectors_hbm, vectors),
            )
        )
    ]
    for load in loads:
        load.start()

    def remote(src, dst, send, recv, to):
        return pltpu.make_async_remote_copy(
            src_ref=src, dst_ref=dst, send_sem=send, recv_sem=recv, device_id=to, device_id_type=MESH
        )

    for load in loads[:3]:
        load.wait()
    q = q_ref[...]
    high = q.astype(BF16)
    low = (q - high.astype(F32)).astype(BF16)
    cube_q[a, :, :384] = jnp.concatenate([high[:, :384], high[:, 384:]], axis=0)
    for h in range(2):
        group_q[h, y, z, c] = jnp.concatenate(
            [high[:, h * 384 : h * 384 + 384], low[:, h * 384 : h * 384 + 384]], axis=0
        )
    owner = owner_ref[...]
    row = row_ref[...].astype(F32)
    lanes = iota((8, 128), 1)
    present = jnp.zeros((8, 128), F32)
    wanted = jnp.zeros((8, 128), F32)
    for k in range(16):
        hit = owner[:, k : k + 1] == lanes
        present = jnp.where(hit, 1.0, present)
        wanted = jnp.where(hit, row[:, k : k + 1], wanted)
    earlier = (iota((8, 8), 1) < iota((8, 8), 0)).astype(BF16)
    rank = jnp.dot(earlier, present.astype(BF16), preferred_element_type=F32)
    slot = (a * 2).astype(F32) + rank
    rows = [
        jnp.sum(jnp.where((present > 0.0) & (rank == float(k)), wanted, 0.0), axis=0, keepdims=True)
        for k in range(2)
    ]
    rows = jnp.concatenate(rows + [jnp.zeros((6, 128), F32)], axis=0)
    upper = jnp.floor(rows * (1.0 / 32.0))
    digits = upper + pltpu.roll(rows - upper * 32.0, 2, 0)
    cube_q[a, :, 384:] = jnp.concatenate(
        [jnp.where(present > 0.0, slot, -1.0), digits], axis=0
    ).astype(BF16)
    place_t[...] = jnp.zeros((128, 128), F32)

    pl.semaphore_wait(barrier, 13)

    cube_copies = []
    for i in range(1, 8):
        _, to = cube_peer(i)
        copy = remote(cube_q.at[a], cube_q.at[a], cq_s.at[i], cq_r.at[i], to)
        copy.start()
        cube_copies.append(copy)

    for i in (2, 1, 3):
        pl.semaphore_signal(plane_sem, inc=1, device_id=line_peer(1, i), device_id_type=MESH)

    first_copies, second_copies = [], []
    for i in (1, 3, 2):
        for h in range(2):
            block = group_q.at[h, y, z, c]
            copy = remote(block, block, g_s.at[h, 0, i], g_r.at[h, 0, i], line_peer(h, i))
            copy.start()
            first_copies.append(copy)

    loads[3].wait()

    def to_book16(i, _):
        pair = book[pl.ds(i * 2, 2)]
        book16[i] = jnp.concatenate([pair[0], pair[1]], axis=0).astype(BF16)
        return 0

    lax.fori_loop(0, 48, to_book16, 0, unroll=8)
    loads[4].wait()

    def decode(l, _):
        for m in range(48):
            for h in range(2):
                span = slice(h * 128, h * 128 + 128)
                index = jnp.concatenate(
                    [
                        jnp.broadcast_to(codes[l, 2 * m : 2 * m + 1, span], (8, 128)),
                        jnp.broadcast_to(codes[l, 2 * m + 1 : 2 * m + 2, span], (8, 128)),
                    ],
                    axis=0,
                )
                near = (index & 127).astype(jnp.int16)
                decoded[l, m * 16 : m * 16 + 16, span] = jnp.where(
                    index < 128,
                    lane_gather(book16[m, :, :128], near),
                    lane_gather(book16[m, :, 128:], near),
                )
        return 0

    lax.fori_loop(0, 6, decode, 0)

    for copy in cube_copies:
        copy.wait_recv()
    pl.semaphore_wait(plane_sem, 3)
    cube = cube_q[...]
    codes_in = cube[:, :, 384:].astype(F32)
    slot_t[...] = jnp.concatenate(
        [codes_in[:, :8].reshape(64, 128), jnp.full((64, 128), -1.0, F32)], axis=0
    ).T
    for k in range(8):
        pair = codes_in[k, 8:10] * 32.0 + codes_in[k, 10:12]
        place_t[pl.ds(pl.multiple_of(w % 8 * 16, 16), 16), :] += jnp.pad(
            pair, ((2 * k, 14 - 2 * k), (0, 0))
        )
    row_t[...] = place_t[...].T
    columns = [cube[:, h * 8 : h * 8 + 8, :384].reshape(64, 384) for h in range(2)]
    columns = jnp.concatenate(columns, axis=1)
    places = iota((16, 128), 0).astype(F32)
    slot_copies = []
    for first in range(0, 16, GROUP):
        group = plane_offsets[first : first + GROUP]
        picks = []
        for dy, dz in group:
            p, _ = plane_peer(dy, dz)
            line = pl.ds(x * 32 + p * 2 + c, 1)
            want_out[dy * 4 + dz] = row_t[line, :]
            picks.append(
                jnp.where(jnp.broadcast_to(slot_t[line, :], (16, 128)) == places, 1.0, 0.0)
            )
        pick = jnp.concatenate(picks, axis=0)[:, :64].astype(BF16)
        chosen = jnp.dot(pick, columns, preferred_element_type=F32).astype(BF16)
        for n, (dy, dz) in enumerate(group):
            k = dy * 4 + dz
            if k == 0:
                slot_in[w] = chosen[n * 16 : n * 16 + 16]
                want_in[w] = want_out[0]
                continue
            slot_out[k] = chosen[n * 16 : n * 16 + 16]
            _, to = plane_peer(dy, dz)
            for copy in (
                remote(want_out.at[k], want_in.at[w], sw_s.at[k], sw_r.at[k], to),
                remote(slot_out.at[k], slot_in.at[w], sq_s.at[k], sq_r.at[k], to),
            ):
                copy.start()
                slot_copies.append(copy)

    lax.fori_loop(6, 8, decode, 0)
    for copy in first_copies:
        copy.wait_recv()
    for i in (1, 3, 2):
        for h in range(2):
            block = group_q.at[h, :, z, c] if h == 0 else group_q.at[h, y, :, c]
            copy = remote(block, block, g_s.at[h, 1, i], g_r.at[h, 1, i], line_peer(1 - h, i))
            copy.start()
            second_copies.append(copy)
    loads[6].wait()

    def to_vectors16(i, _):
        span = pl.ds(pl.multiple_of(i * 128, 128), 128)
        vectors16[span, :] = vectors[span, :].astype(BF16)
        return 0

    lax.fori_loop(0, 8, to_vectors16, 0)

    for copy in slot_copies:
        copy.wait_recv()
    slots = slot_in[...].reshape(256, 768)
    ids = jnp.concatenate(
        [jnp.sum(want_in[b * 8 : b * 8 + 8], axis=0) for b in range(2)], axis=1
    ).astype(I32)
    found = jnp.zeros((256, 256), F32)
    for b in range(4):
        part = lax.dot_general(
            vectors16[b * 256 : b * 256 + 256, :],
            slots,
            (((1,), (1,)), ((), ())),
            preferred_element_type=F32,
        )
        found = jnp.where(iota((256, 256), 0) + b * 256 == ids, part, found)
    scored = jnp.sum(found, axis=0, keepdims=True)
    for b in range(2):
        score_out[b] = scored[:, b * 128 : b * 128 + 128]
    score_in[me] = score_out[w // 8]
    offsets = [(dx, dy, dz, dc) for dx in range(4) for dy in range(4) for dz in range(4) for dc in range(2)]
    offsets.sort(key=lambda o: -sum(min(d, 4 - d) for d in o[:3]))
    offsets.remove((0, 0, 0, 0))
    for dx, dy, dz, dc in offsets:
        p = (y + dy) % 4 * 4 + (z + dz) % 4
        to = {"group": (x + dx) % 4, "shard": p * 2 + (c + dc) % 2}
        remote(score_out.at[p // 8], score_in.at[me], rs_s.at[0], rs_r.at[0], to).start()

    for copy in second_copies:
        copy.wait_recv()
    sibling = device(x, y, z, 1 - c)
    core_copies = []
    for h in range(2):
        block = group_q.at[h, :, :, c]
        copy = remote(block, block, g_s.at[h, 2, 0], g_r.at[h, 2, 0], sibling)
        copy.start()
        core_copies.append(copy)
    for copy in core_copies:
        copy.wait_recv()

    loads[5].wait()
    probes = probes_ref[...]

    def score_list(l, _):
        left = jnp.concatenate(
            [group_q[0].reshape(512, 384), group_q[1].reshape(512, 384)], axis=1
        )
        both = jnp.dot(left, decoded[l], preferred_element_type=F32).reshape(32, 2, 8, 256)
        sums = (both[:, 0] + both[:, 1]).reshape(256, 256)
        probed = jnp.max(jnp.where(probes == s * 8 + l, 1.0, 0.0), axis=0, keepdims=True)
        pq_ref[l] = jnp.where(probed > 0.0, sums.T, 0.0)
        return 0

    lax.fori_loop(0, 8, score_list, 0, unroll=2)

    everyone = score_in.at[pl.ds(0, 127)]
    pltpu.make_async_copy(everyone, everyone, rs_r.at[0]).wait()
    total[...] = score_in[...].reshape(128, 128).T
    line = w % 8 * 16 + a * 2
    own = jnp.where(rank < 0.5, total[pl.ds(line, 1), :], total[pl.ds(line + 1, 1), :])
    result = jnp.zeros((8, 16), F32)
    for k in range(16):
        value = jnp.sum(
            jnp.where(owner[:, k : k + 1] == lanes, own, 0.0), axis=1, keepdims=True
        )
        result = jnp.where(iota((8, 16), 1) == k, value, result)
    rr_ref[...] = result

    for copy in (
        cube_copies + first_copies + second_copies + core_copies + slot_copies
    ):
        copy.wait_send()
    pltpu.make_async_copy(everyone, everyone, rs_s.at[0]).wait()


def hand_over(pq_in, rr_in, pq_ref, rr_ref, sems):
    copies = [pltpu.make_async_copy(rr_in, rr_ref, sems.at[8])]
    copies += [pltpu.make_async_copy(pq_in.at[i], pq_ref.at[i], sems.at[i]) for i in range(8)]
    for copy in copies:
        copy.start()
    for copy in copies:
        copy.wait()


def per_device(queries, codebook, pq_codes, probes, vectors, cand_owner, cand_row):
    vmem = pl.BlockSpec(memory_space=pltpu.VMEM)
    hbm = pl.BlockSpec(memory_space=pltpu.HBM)
    dma = pltpu.SemaphoreType.DMA
    outs = (
        jax.ShapeDtypeStruct((8, 256, 256), F32),
        jax.ShapeDtypeStruct((8, 16), F32),
    )
    held = pl.pallas_call(
        kernel,
        out_shape=outs,
        in_specs=[hbm] * 7,
        out_specs=(vmem, vmem),
        scratch_shapes=[
            pltpu.VMEM((8, 768), F32),
            pltpu.VMEM((8, 256), I32),
            pltpu.VMEM((8, 16), I32),
            pltpu.VMEM((8, 16), I32),
            pltpu.VMEM((8, 96, 256), I32),
            pltpu.VMEM((96, 8, 256), F32),
            pltpu.VMEM((1024, 768), F32),
            pltpu.VMEM((48, 16, 256), BF16),
            pltpu.VMEM((1024, 768), BF16),
            pltpu.VMEM((8, 768, 256), BF16),
            pltpu.VMEM((2, 4, 4, 2, 16, 384), BF16),
            pltpu.VMEM((8, 16, 512), BF16),
            pltpu.VMEM((128, 128), F32),
            pltpu.VMEM((128, 128), F32),
            pltpu.VMEM((128, 128), F32),
            pltpu.VMEM((16, 1, 128), F32),
            pltpu.VMEM((16, 1, 128), F32),
            pltpu.VMEM((16, 16, 768), BF16),
            pltpu.VMEM((16, 16, 768), BF16),
            pltpu.VMEM((2, 1, 128), F32),
            pltpu.VMEM((128, 1, 128), F32),
            pltpu.VMEM((128, 128), F32),
            dma((7,)),
            pltpu.SemaphoreType.REGULAR,
            dma((8,)), dma((8,)),
            dma((2, 3, 4)), dma((2, 3, 4)),
            dma((16,)), dma((16,)), dma((16,)), dma((16,)),
            dma((1,)), dma((1,)),
        ],
        compiler_params=pltpu.CompilerParams(
            vmem_limit_bytes=32 << 20, collective_id=0, has_side_effects=True
        ),
        cost_estimate=pl.CostEstimate(flops=3_000_000_000, bytes_accessed=7_000_000, transcendentals=0),
        name="search",
    )(
        *(
            pltpu.with_memory_space_constraint(operand, pltpu.HBM)
            for operand in (
                queries,
                probes.T,
                cand_owner,
                cand_row,
                pq_codes,
                codebook.transpose(0, 2, 1),
                vectors,
            )
        )
    )
    return pl.pallas_call(
        hand_over,
        out_shape=outs,
        in_specs=[pl.BlockSpec(memory_space=pl.ANY)] * 2,
        out_specs=(hbm, hbm),
        scratch_shapes=[dma((9,))],
        compiler_params=pltpu.CompilerParams(vmem_limit_bytes=16 << 20),
        name="hand_over",
    )(*held)


def solution(mesh):
    both = ("group", "shard")
    in_specs = (
        P(both, None),
        P(),
        P(both, None, None),
        P("group", None),
        P(both, None),
        P(both, None),
        P(both, None),
    )
    out_specs = (P(both, None, None), P(both, None))
    return jax.shard_map(
        per_device, mesh=mesh, in_specs=in_specs, out_specs=out_specs, check_vma=False
    )
```

```python
import jax
import jax.numpy as jnp
from jax import lax
from jax.experimental import pallas as pl
from jax.experimental.pallas import tpu as pltpu
from jax.sharding import PartitionSpec as P

MESH = pl.DeviceIdType.MESH
F32, BF16, I32 = jnp.float32, jnp.bfloat16, jnp.int32
GROUP = 16


def lane_gather(table, index):
    numbers = lax.GatherDimensionNumbers(
        offset_dims=(),
        collapsed_slice_dims=(1,),
        start_index_map=(1,),
        operand_batching_dims=(0,),
        start_indices_batching_dims=(0,),
    )
    return lax.gather(
        table, index[..., None], numbers, (1, 1), mode=lax.GatherScatterMode.PROMISE_IN_BOUNDS
    )


def iota(shape, dim):
    return lax.broadcasted_iota(I32, shape, dim)


def kernel(
    q_hbm,
    probes_hbm,
    owner_hbm,
    row_hbm,
    codes_hbm,
    book_hbm,
    vectors_hbm,
    pq_ref,
    rr_ref,
    q_ref,
    probes_ref,
    owner_ref,
    row_ref,
    codes,
    book,
    vectors,
    book16,
    vectors16,
    decoded,
    group_q,
    cube_q,
    slot_t,
    place_t,
    row_t,
    want_out,
    want_in,
    slot_out,
    slot_in,
    score_out,
    score_in,
    total,
    load_sem,
    plane_sem,
    cq_s, cq_r,
    g_s, g_r,
    sq_s, sq_r, sw_s, sw_r,
    rs_s, rs_r,
):
    x = lax.axis_index("group")
    s = lax.axis_index("shard")
    y, z, c = s // 8, (s // 2) % 4, s % 2
    me = x * 32 + s
    a = x * 2 + c
    w = y * 4 + z

    def device(x, y, z, c):
        return {"group": x, "shard": (y * 4 + z) * 2 + c}

    def cube_peer(i):
        p = (a + i) % 8
        return p, device(p // 2, y, z, p % 2)

    def plane_peer(dy, dz):
        to_y, to_z = (y + dy) % 4, (z + dz) % 4
        return to_y * 4 + to_z, device(x, to_y, to_z, c)

    plane_offsets = [(dy, dz) for dy in range(4) for dz in range(4)]
    plane_offsets.sort(key=lambda o: -sum(min(d, 4 - d) for d in o))

    def line_peer(axis, i):
        return (
            device(x, (y + i) % 4, z, c) if axis == 0 else device(x, y, (z + i) % 4, c)
        )

    barrier = pltpu.get_barrier_semaphore()
    for i in (2, 1, 3):
        for axis in range(2):
            pl.semaphore_signal(barrier, inc=1, device_id=line_peer(axis, i), device_id_type=MESH)
    for i in (4, 5, 2, 3, 6, 7, 1):
        pl.semaphore_signal(barrier, inc=1, device_id=cube_peer(i)[1], device_id_type=MESH)

    loads = [
        pltpu.make_async_copy(src, dst, load_sem.at[i])
        for i, (src, dst) in enumerate(
            (
                (q_hbm, q_ref),
                (owner_hbm, owner_ref),
                (row_hbm, row_ref),
                (book_hbm, book),
                (codes_hbm, codes),
                (probes_hbm, probes_ref),
                (vectors_hbm, vectors),
            )
        )
    ]
    for load in loads:
        load.start()

    def remote(src, dst, send, recv, to):
        return pltpu.make_async_remote_copy(
            src_ref=src, dst_ref=dst, send_sem=send, recv_sem=recv, device_id=to, device_id_type=MESH
        )

    for load in loads[:3]:
        load.wait()
    q = q_ref[...]
    high = q.astype(BF16)
    low = (q - high.astype(F32)).astype(BF16)
    cube_q[a, :, :384] = jnp.concatenate([high[:, :384], high[:, 384:]], axis=0)
    for h in range(2):
        group_q[h, y, z, c] = jnp.concatenate(
            [high[:, h * 384 : h * 384 + 384], low[:, h * 384 : h * 384 + 384]], axis=0
        )
    owner = owner_ref[...]
    row = row_ref[...].astype(F32)
    lanes = iota((8, 128), 1)
    present = jnp.zeros((8, 128), F32)
    wanted = jnp.zeros((8, 128), F32)
    for k in range(16):
        hit = owner[:, k : k + 1] == lanes
        present = jnp.where(hit, 1.0, present)
        wanted = jnp.where(hit, row[:, k : k + 1], wanted)
    earlier = (iota((8, 8), 1) < iota((8, 8), 0)).astype(BF16)
    rank = jnp.dot(earlier, present.astype(BF16), preferred_element_type=F32)
    slot = (a * 2).astype(F32) + rank
    rows = [
        jnp.sum(jnp.where((present > 0.0) & (rank == float(k)), wanted, 0.0), axis=0, keepdims=True)
        for k in range(2)
    ]
    rows = jnp.concatenate(rows + [jnp.zeros((6, 128), F32)], axis=0)
    upper = jnp.floor(rows * (1.0 / 32.0))
    digits = upper + pltpu.roll(rows - upper * 32.0, 2, 0)
    cube_q[a, :, 384:] = jnp.concatenate(
        [jnp.where(present > 0.0, slot, -1.0), digits], axis=0
    ).astype(BF16)
    place_t[...] = jnp.zeros((128, 128), F32)

    pl.semaphore_wait(barrier, 13)

    cube_copies = []
    for i in (4, 5, 3, 2, 6, 7, 1):
        _, to = cube_peer(i)
        copy = remote(cube_q.at[a], cube_q.at[a], cq_s.at[i], cq_r.at[i], to)
        copy.start()
        cube_copies.append(copy)

    for i in (2, 1, 3):
        pl.semaphore_signal(plane_sem, inc=1, device_id=line_peer(1, i), device_id_type=MESH)

    first_copies, second_copies = [], []
    for i in (1, 3, 2):
        for h in range(2):
            block = group_q.at[h, y, z, c]
            copy = remote(block, block, g_s.at[h, 0, i], g_r.at[h, 0, i], line_peer(h, i))
            copy.start()
            first_copies.append(copy)

    loads[3].wait()

    def to_book16(i, _):
        pair = book[pl.ds(i * 2, 2)]
        book16[i] = jnp.concatenate([pair[0], pair[1]], axis=0).astype(BF16)
        return 0

    lax.fori_loop(0, 48, to_book16, 0, unroll=8)
    loads[4].wait()

    def decode(l, _):
        for m in range(48):
            for h in range(2):
                span = slice(h * 128, h * 128 + 128)
                index = jnp.concatenate(
                    [
                        jnp.broadcast_to(codes[l, 2 * m : 2 * m + 1, span], (8, 128)),
                        jnp.broadcast_to(codes[l, 2 * m + 1 : 2 * m + 2, span], (8, 128)),
                    ],
                    axis=0,
                )
                near = (index & 127).astype(jnp.int16)
                decoded[l, m * 16 : m * 16 + 16, span] = jnp.where(
                    index < 128,
                    lane_gather(book16[m, :, :128], near),
                    lane_gather(book16[m, :, 128:], near),
                )
        return 0

    lax.fori_loop(0, 6, decode, 0)

    for copy in cube_copies:
        copy.wait_recv()
    pl.semaphore_wait(plane_sem, 3)
    cube = cube_q[...]
    codes_in = cube[:, :, 384:].astype(F32)
    slot_t[...] = jnp.concatenate(
        [codes_in[:, :8].reshape(64, 128), jnp.full((64, 128), -1.0, F32)], axis=0
    ).T
    for k in range(8):
        pair = codes_in[k, 8:10] * 32.0 + codes_in[k, 10:12]
        place_t[pl.ds(pl.multiple_of(w % 8 * 16, 16), 16), :] += jnp.pad(
            pair, ((2 * k, 14 - 2 * k), (0, 0))
        )
    row_t[...] = place_t[...].T
    slot_copies = []
    for dy, dz in plane_offsets:
        k = dy * 4 + dz
        p, to = plane_peer(dy, dz)
        want_out[k] = row_t[pl.ds(x * 32 + p * 2 + c, 1), :]
        if k == 0:
            want_in[w] = want_out[0]
            continue
        copy = remote(want_out.at[k], want_in.at[w], sw_s.at[k], sw_r.at[k], to)
        copy.start()
        slot_copies.append(copy)
    columns = [cube[:, h * 8 : h * 8 + 8, :384].reshape(64, 384) for h in range(2)]
    columns = jnp.concatenate(columns, axis=1)
    places = iota((16, 128), 0).astype(F32)
    for first in range(0, 16, GROUP):
        group = plane_offsets[first : first + GROUP]
        picks = []
        for dy, dz in group:
            p, _ = plane_peer(dy, dz)
            line = pl.ds(x * 32 + p * 2 + c, 1)
            picks.append(
                jnp.where(jnp.broadcast_to(slot_t[line, :], (16, 128)) == places, 1.0, 0.0)
            )
        pick = jnp.concatenate(picks, axis=0)[:, :64].astype(BF16)
        chosen = jnp.dot(pick, columns, preferred_element_type=F32).astype(BF16)
        for n, (dy, dz) in enumerate(group):
            k = dy * 4 + dz
            if k == 0:
                slot_in[w] = chosen[n * 16 : n * 16 + 16]
                continue
            slot_out[k] = chosen[n * 16 : n * 16 + 16]
            _, to = plane_peer(dy, dz)
            copy = remote(slot_out.at[k], slot_in.at[w], sq_s.at[k], sq_r.at[k], to)
            copy.start()
            slot_copies.append(copy)

    lax.fori_loop(6, 8, decode, 0)
    for copy in first_copies:
        copy.wait_recv()
    for i in (1, 3, 2):
        for h in range(2):
            block = group_q.at[h, :, z, c] if h == 0 else group_q.at[h, y, :, c]
            copy = remote(block, block, g_s.at[h, 1, i], g_r.at[h, 1, i], line_peer(1 - h, i))
            copy.start()
            second_copies.append(copy)
    loads[6].wait()

    def to_vectors16(i, _):
        span = pl.ds(pl.multiple_of(i * 128, 128), 128)
        vectors16[span, :] = vectors[span, :].astype(BF16)
        return 0

    lax.fori_loop(0, 8, to_vectors16, 0)

    for copy in slot_copies:
        copy.wait_recv()
    slots = slot_in[...].reshape(256, 768)
    ids = jnp.concatenate(
        [jnp.sum(want_in[b * 8 : b * 8 + 8], axis=0) for b in range(2)], axis=1
    ).astype(I32)
    found = jnp.zeros((256, 256), F32)
    for b in range(4):
        part = lax.dot_general(
            vectors16[b * 256 : b * 256 + 256, :],
            slots,
            (((1,), (1,)), ((), ())),
            preferred_element_type=F32,
        )
        found = jnp.where(iota((256, 256), 0) + b * 256 == ids, part, found)
    scored = jnp.sum(found, axis=0, keepdims=True)
    for b in range(2):
        score_out[b] = scored[:, b * 128 : b * 128 + 128]
    score_in[me] = score_out[w // 8]
    offsets = [(dx, dy, dz, dc) for dx in range(4) for dy in range(4) for dz in range(4) for dc in range(2)]
    offsets.sort(key=lambda o: -sum(min(d, 4 - d) for d in o[:3]))
    offsets.remove((0, 0, 0, 0))
    for dx, dy, dz, dc in offsets:
        p = (y + dy) % 4 * 4 + (z + dz) % 4
        to = {"group": (x + dx) % 4, "shard": p * 2 + (c + dc) % 2}
        remote(score_out.at[p // 8], score_in.at[me], rs_s.at[0], rs_r.at[0], to).start()

    for copy in second_copies:
        copy.wait_recv()
    sibling = device(x, y, z, 1 - c)
    core_copies = []
    for h in range(2):
        block = group_q.at[h, :, :, c]
        copy = remote(block, block, g_s.at[h, 2, 0], g_r.at[h, 2, 0], sibling)
        copy.start()
        core_copies.append(copy)
    for copy in core_copies:
        copy.wait_recv()

    loads[5].wait()
    probes = probes_ref[...]

    def score_list(l, _):
        left = jnp.concatenate(
            [group_q[0].reshape(512, 384), group_q[1].reshape(512, 384)], axis=1
        )
        both = jnp.dot(left, decoded[l], preferred_element_type=F32).reshape(32, 2, 8, 256)
        sums = (both[:, 0] + both[:, 1]).reshape(256, 256)
        probed = jnp.max(jnp.where(probes == s * 8 + l, 1.0, 0.0), axis=0, keepdims=True)
        pq_ref[l] = jnp.where(probed > 0.0, sums.T, 0.0)
        return 0

    lax.fori_loop(0, 8, score_list, 0, unroll=2)

    everyone = score_in.at[pl.ds(0, 127)]
    pltpu.make_async_copy(everyone, everyone, rs_r.at[0]).wait()
    total[...] = score_in[...].reshape(128, 128).T
    line = w % 8 * 16 + a * 2
    own = jnp.where(rank < 0.5, total[pl.ds(line, 1), :], total[pl.ds(line + 1, 1), :])
    result = jnp.zeros((8, 16), F32)
    for k in range(16):
        value = jnp.sum(
            jnp.where(owner[:, k : k + 1] == lanes, own, 0.0), axis=1, keepdims=True
        )
        result = jnp.where(iota((8, 16), 1) == k, value, result)
    rr_ref[...] = result

    for copy in (
        cube_copies + first_copies + second_copies + core_copies + slot_copies
    ):
        copy.wait_send()
    pltpu.make_async_copy(everyone, everyone, rs_s.at[0]).wait()


def hand_over(pq_in, rr_in, pq_ref, rr_ref, sems):
    copies = [pltpu.make_async_copy(rr_in, rr_ref, sems.at[8])]
    copies += [pltpu.make_async_copy(pq_in.at[i], pq_ref.at[i], sems.at[i]) for i in range(8)]
    for copy in copies:
        copy.start()
    for copy in copies:
        copy.wait()


def per_device(queries, codebook, pq_codes, probes, vectors, cand_owner, cand_row):
    vmem = pl.BlockSpec(memory_space=pltpu.VMEM)
    hbm = pl.BlockSpec(memory_space=pltpu.HBM)
    dma = pltpu.SemaphoreType.DMA
    outs = (
        jax.ShapeDtypeStruct((8, 256, 256), F32),
        jax.ShapeDtypeStruct((8, 16), F32),
    )
    held = pl.pallas_call(
        kernel,
        out_shape=outs,
        in_specs=[hbm] * 7,
        out_specs=(vmem, vmem),
        scratch_shapes=[
            pltpu.VMEM((8, 768), F32),
            pltpu.VMEM((8, 256), I32),
            pltpu.VMEM((8, 16), I32),
            pltpu.VMEM((8, 16), I32),
            pltpu.VMEM((8, 96, 256), I32),
            pltpu.VMEM((96, 8, 256), F32),
            pltpu.VMEM((1024, 768), F32),
            pltpu.VMEM((48, 16, 256), BF16),
            pltpu.VMEM((1024, 768), BF16),
            pltpu.VMEM((8, 768, 256), BF16),
            pltpu.VMEM((2, 4, 4, 2, 16, 384), BF16),
            pltpu.VMEM((8, 16, 512), BF16),
            pltpu.VMEM((128, 128), F32),
            pltpu.VMEM((128, 128), F32),
            pltpu.VMEM((128, 128), F32),
            pltpu.VMEM((16, 1, 128), F32),
            pltpu.VMEM((16, 1, 128), F32),
            pltpu.VMEM((16, 16, 768), BF16),
            pltpu.VMEM((16, 16, 768), BF16),
            pltpu.VMEM((2, 1, 128), F32),
            pltpu.VMEM((128, 1, 128), F32),
            pltpu.VMEM((128, 128), F32),
            dma((7,)),
            pltpu.SemaphoreType.REGULAR,
            dma((8,)), dma((8,)),
            dma((2, 3, 4)), dma((2, 3, 4)),
            dma((16,)), dma((16,)), dma((16,)), dma((16,)),
            dma((1,)), dma((1,)),
        ],
        compiler_params=pltpu.CompilerParams(
            vmem_limit_bytes=32 << 20, collective_id=0, has_side_effects=True
        ),
        cost_estimate=pl.CostEstimate(flops=3_000_000_000, bytes_accessed=7_000_000, transcendentals=0),
        name="search",
    )(
        *(
            pltpu.with_memory_space_constraint(operand, pltpu.HBM)
            for operand in (
                queries,
                probes.T,
                cand_owner,
                cand_row,
                pq_codes,
                codebook.transpose(0, 2, 1),
                vectors,
            )
        )
    )
    return pl.pallas_call(
        hand_over,
        out_shape=outs,
        in_specs=[pl.BlockSpec(memory_space=pl.ANY)] * 2,
        out_specs=(hbm, hbm),
        scratch_shapes=[dma((9,))],
        compiler_params=pltpu.CompilerParams(vmem_limit_bytes=16 << 20),
        name="hand_over",
    )(*held)


def solution(mesh):
    both = ("group", "shard")
    in_specs = (
        P(both, None),
        P(),
        P(both, None, None),
        P("group", None),
        P(both, None),
        P(both, None),
        P(both, None),
    )
    out_specs = (P(both, None, None), P(both, None))
    return jax.shard_map(
        per_device, mesh=mesh, in_specs=in_specs, out_specs=out_specs, check_vma=False
    )
```

```python
import jax
import jax.numpy as jnp
from jax import lax
from jax.experimental import pallas as pl
from jax.experimental.pallas import tpu as pltpu
from jax.sharding import PartitionSpec as P

MESH = pl.DeviceIdType.MESH
F32, BF16, I32 = jnp.float32, jnp.bfloat16, jnp.int32
GROUP = 16


def lane_gather(table, index):
    numbers = lax.GatherDimensionNumbers(
        offset_dims=(),
        collapsed_slice_dims=(1,),
        start_index_map=(1,),
        operand_batching_dims=(0,),
        start_indices_batching_dims=(0,),
    )
    return lax.gather(
        table, index[..., None], numbers, (1, 1), mode=lax.GatherScatterMode.PROMISE_IN_BOUNDS
    )


def iota(shape, dim):
    return lax.broadcasted_iota(I32, shape, dim)


def kernel(
    q_hbm,
    probes_hbm,
    owner_hbm,
    row_hbm,
    codes_hbm,
    book_hbm,
    vectors_hbm,
    pq_ref,
    rr_ref,
    q_ref,
    probes_ref,
    owner_ref,
    row_ref,
    codes,
    book,
    vectors,
    book16,
    vectors16,
    decoded,
    group_q,
    cube_q,
    cube_w,
    slot_t,
    place_t,
    row_t,
    want_out,
    want_in,
    slot_out,
    slot_in,
    score_out,
    score_in,
    total,
    load_sem,
    plane_sem,
    cq_s, cq_r, cw_s, cw_r,
    g_s, g_r,
    sq_s, sq_r, sw_s, sw_r,
    rs_s, rs_r,
):
    x = lax.axis_index("group")
    s = lax.axis_index("shard")
    y, z, c = s // 8, (s // 2) % 4, s % 2
    me = x * 32 + s
    a = x * 2 + c
    w = y * 4 + z

    def device(x, y, z, c):
        return {"group": x, "shard": (y * 4 + z) * 2 + c}

    def cube_peer(i):
        p = (a + i) % 8
        return p, device(p // 2, y, z, p % 2)

    def plane_peer(dy, dz):
        to_y, to_z = (y + dy) % 4, (z + dz) % 4
        return to_y * 4 + to_z, device(x, to_y, to_z, c)

    plane_offsets = [(dy, dz) for dy in range(4) for dz in range(4)]
    plane_offsets.sort(key=lambda o: -sum(min(d, 4 - d) for d in o))

    def line_peer(axis, i):
        return (
            device(x, (y + i) % 4, z, c) if axis == 0 else device(x, y, (z + i) % 4, c)
        )

    barrier = pltpu.get_barrier_semaphore()
    for i in (2, 1, 3):
        for axis in range(2):
            pl.semaphore_signal(barrier, inc=1, device_id=line_peer(axis, i), device_id_type=MESH)
    for i in (4, 5, 2, 3, 6, 7, 1):
        pl.semaphore_signal(barrier, inc=1, device_id=cube_peer(i)[1], device_id_type=MESH)

    loads = [
        pltpu.make_async_copy(src, dst, load_sem.at[i])
        for i, (src, dst) in enumerate(
            (
                (q_hbm, q_ref),
                (owner_hbm, owner_ref),
                (row_hbm, row_ref),
                (book_hbm, book),
                (codes_hbm, codes),
                (probes_hbm, probes_ref),
                (vectors_hbm, vectors),
            )
        )
    ]
    for load in loads:
        load.start()

    def remote(src, dst, send, recv, to):
        return pltpu.make_async_remote_copy(
            src_ref=src, dst_ref=dst, send_sem=send, recv_sem=recv, device_id=to, device_id_type=MESH
        )

    for load in loads[:3]:
        load.wait()
    q = q_ref[...]
    high = q.astype(BF16)
    low = (q - high.astype(F32)).astype(BF16)
    cube_q[a] = jnp.concatenate([high[:, :384], high[:, 384:]], axis=0)
    for h in range(2):
        group_q[h, y, z, c] = jnp.concatenate(
            [high[:, h * 384 : h * 384 + 384], low[:, h * 384 : h * 384 + 384]], axis=0
        )
    owner = owner_ref[...]
    row = row_ref[...].astype(F32)
    lanes = iota((8, 128), 1)
    present = jnp.zeros((8, 128), F32)
    wanted = jnp.zeros((8, 128), F32)
    for k in range(16):
        hit = owner[:, k : k + 1] == lanes
        present = jnp.where(hit, 1.0, present)
        wanted = jnp.where(hit, row[:, k : k + 1], wanted)
    earlier = (iota((8, 8), 1) < iota((8, 8), 0)).astype(BF16)
    rank = jnp.dot(earlier, present.astype(BF16), preferred_element_type=F32)
    slot = (a * 2).astype(F32) + rank
    rows = [
        jnp.sum(jnp.where((present > 0.0) & (rank == float(k)), wanted, 0.0), axis=0, keepdims=True)
        for k in range(2)
    ]
    rows = jnp.concatenate(rows + [jnp.zeros((6, 128), F32)], axis=0)
    upper = jnp.floor(rows * (1.0 / 32.0))
    digits = upper + pltpu.roll(rows - upper * 32.0, 2, 0)
    cube_w[a] = jnp.concatenate(
        [jnp.where(present > 0.0, slot, -1.0), digits], axis=0
    ).astype(BF16)
    place_t[...] = jnp.zeros((128, 128), F32)

    pl.semaphore_wait(barrier, 13)

    cube_copies, wish_copies = [], []
    for block, send, recv, copies in (
        (cube_w.at[a], cw_s, cw_r, wish_copies),
        (cube_q.at[a], cq_s, cq_r, cube_copies),
    ):
        for i in (4, 5, 3, 2, 6, 7, 1):
            copy = remote(block, block, send.at[i], recv.at[i], cube_peer(i)[1])
            copy.start()
            copies.append(copy)

    for i in (2, 1, 3):
        pl.semaphore_signal(plane_sem, inc=1, device_id=line_peer(1, i), device_id_type=MESH)

    first_copies, second_copies = [], []
    for i in (1, 3, 2):
        for h in range(2):
            block = group_q.at[h, y, z, c]
            copy = remote(block, block, g_s.at[h, 0, i], g_r.at[h, 0, i], line_peer(h, i))
            copy.start()
            first_copies.append(copy)

    loads[3].wait()

    def to_book16(i, _):
        pair = book[pl.ds(i * 2, 2)]
        book16[i] = jnp.concatenate([pair[0], pair[1]], axis=0).astype(BF16)
        return 0

    lax.fori_loop(0, 48, to_book16, 0, unroll=8)
    loads[4].wait()

    def decode(l, _):
        for m in range(48):
            for h in range(2):
                span = slice(h * 128, h * 128 + 128)
                index = jnp.concatenate(
                    [
                        jnp.broadcast_to(codes[l, 2 * m : 2 * m + 1, span], (8, 128)),
                        jnp.broadcast_to(codes[l, 2 * m + 1 : 2 * m + 2, span], (8, 128)),
                    ],
                    axis=0,
                )
                near = (index & 127).astype(jnp.int16)
                decoded[l, m * 16 : m * 16 + 16, span] = jnp.where(
                    index < 128,
                    lane_gather(book16[m, :, :128], near),
                    lane_gather(book16[m, :, 128:], near),
                )
        return 0

    lax.fori_loop(0, 6, decode, 0)

    for copy in wish_copies:
        copy.wait_recv()
    pl.semaphore_wait(plane_sem, 3)
    codes_in = cube_w[...].astype(F32)
    slot_t[...] = jnp.concatenate(
        [codes_in[:, :8].reshape(64, 128), jnp.full((64, 128), -1.0, F32)], axis=0
    ).T
    for k in range(8):
        pair = codes_in[k, 8:10] * 32.0 + codes_in[k, 10:12]
        place_t[pl.ds(pl.multiple_of(w % 8 * 16, 16), 16), :] += jnp.pad(
            pair, ((2 * k, 14 - 2 * k), (0, 0))
        )
    row_t[...] = place_t[...].T
    slot_copies = []
    for dy, dz in plane_offsets:
        k = dy * 4 + dz
        p, to = plane_peer(dy, dz)
        want_out[k] = row_t[pl.ds(x * 32 + p * 2 + c, 1), :]
        if k == 0:
            want_in[w] = want_out[0]
            continue
        copy = remote(want_out.at[k], want_in.at[w], sw_s.at[k], sw_r.at[k], to)
        copy.start()
        slot_copies.append(copy)
    places = iota((16, 128), 0).astype(F32)
    picks = []
    for dy, dz in plane_offsets:
        p, _ = plane_peer(dy, dz)
        line = jnp.broadcast_to(slot_t[pl.ds(x * 32 + p * 2 + c, 1), :], (16, 128))
        picks.append(jnp.where(line == places, 1.0, 0.0))
    pick_all = jnp.concatenate(picks, axis=0)[:, :64].astype(BF16)
    for copy in cube_copies:
        copy.wait_recv()
    cube = cube_q[...]
    columns = [cube[:, h * 8 : h * 8 + 8, :].reshape(64, 384) for h in range(2)]
    columns = jnp.concatenate(columns, axis=1)
    for first in range(0, 16, GROUP):
        group = plane_offsets[first : first + GROUP]
        pick = pick_all[first * 16 : (first + GROUP) * 16]
        chosen = jnp.dot(pick, columns, preferred_element_type=F32).astype(BF16)
        for n, (dy, dz) in enumerate(group):
            k = dy * 4 + dz
            if k == 0:
                slot_in[w] = chosen[n * 16 : n * 16 + 16]
                continue
            slot_out[k] = chosen[n * 16 : n * 16 + 16]
            _, to = plane_peer(dy, dz)
            copy = remote(slot_out.at[k], slot_in.at[w], sq_s.at[k], sq_r.at[k], to)
            copy.start()
            slot_copies.append(copy)

    lax.fori_loop(6, 8, decode, 0)
    for copy in first_copies:
        copy.wait_recv()
    for i in (1, 3, 2):
        for h in range(2):
            block = group_q.at[h, :, z, c] if h == 0 else group_q.at[h, y, :, c]
            copy = remote(block, block, g_s.at[h, 1, i], g_r.at[h, 1, i], line_peer(1 - h, i))
            copy.start()
            second_copies.append(copy)
    loads[6].wait()

    def to_vectors16(i, _):
        span = pl.ds(pl.multiple_of(i * 128, 128), 128)
        vectors16[span, :] = vectors[span, :].astype(BF16)
        return 0

    lax.fori_loop(0, 8, to_vectors16, 0)

    for copy in slot_copies:
        copy.wait_recv()
    slots = slot_in[...].reshape(256, 768)
    ids = jnp.concatenate(
        [jnp.sum(want_in[b * 8 : b * 8 + 8], axis=0) for b in range(2)], axis=1
    ).astype(I32)
    found = jnp.zeros((256, 256), F32)
    for b in range(4):
        part = lax.dot_general(
            vectors16[b * 256 : b * 256 + 256, :],
            slots,
            (((1,), (1,)), ((), ())),
            preferred_element_type=F32,
        )
        found = jnp.where(iota((256, 256), 0) + b * 256 == ids, part, found)
    scored = jnp.sum(found, axis=0, keepdims=True)
    for b in range(2):
        score_out[b] = scored[:, b * 128 : b * 128 + 128]
    score_in[me] = score_out[w // 8]
    offsets = [(dx, dy, dz, dc) for dx in range(4) for dy in range(4) for dz in range(4) for dc in range(2)]
    offsets.sort(key=lambda o: -sum(min(d, 4 - d) for d in o[:3]))
    offsets.remove((0, 0, 0, 0))
    for dx, dy, dz, dc in offsets:
        p = (y + dy) % 4 * 4 + (z + dz) % 4
        to = {"group": (x + dx) % 4, "shard": p * 2 + (c + dc) % 2}
        remote(score_out.at[p // 8], score_in.at[me], rs_s.at[0], rs_r.at[0], to).start()

    for copy in second_copies:
        copy.wait_recv()
    sibling = device(x, y, z, 1 - c)
    core_copies = []
    for h in range(2):
        block = group_q.at[h, :, :, c]
        copy = remote(block, block, g_s.at[h, 2, 0], g_r.at[h, 2, 0], sibling)
        copy.start()
        core_copies.append(copy)
    for copy in core_copies:
        copy.wait_recv()

    loads[5].wait()
    probes = probes_ref[...]

    def score_list(l, _):
        left = jnp.concatenate(
            [group_q[0].reshape(512, 384), group_q[1].reshape(512, 384)], axis=1
        )
        both = jnp.dot(left, decoded[l], preferred_element_type=F32).reshape(32, 2, 8, 256)
        sums = (both[:, 0] + both[:, 1]).reshape(256, 256)
        probed = jnp.max(jnp.where(probes == s * 8 + l, 1.0, 0.0), axis=0, keepdims=True)
        pq_ref[l] = jnp.where(probed > 0.0, sums.T, 0.0)
        return 0

    lax.fori_loop(0, 8, score_list, 0, unroll=2)

    everyone = score_in.at[pl.ds(0, 127)]
    pltpu.make_async_copy(everyone, everyone, rs_r.at[0]).wait()
    total[...] = score_in[...].reshape(128, 128).T
    line = w % 8 * 16 + a * 2
    own = jnp.where(rank < 0.5, total[pl.ds(line, 1), :], total[pl.ds(line + 1, 1), :])
    result = jnp.zeros((8, 16), F32)
    for k in range(16):
        value = jnp.sum(
            jnp.where(owner[:, k : k + 1] == lanes, own, 0.0), axis=1, keepdims=True
        )
        result = jnp.where(iota((8, 16), 1) == k, value, result)
    rr_ref[...] = result

    for copy in (
        wish_copies + cube_copies + first_copies + second_copies + core_copies + slot_copies
    ):
        copy.wait_send()
    pltpu.make_async_copy(everyone, everyone, rs_s.at[0]).wait()


def hand_over(pq_in, rr_in, pq_ref, rr_ref, sems):
    copies = [pltpu.make_async_copy(rr_in, rr_ref, sems.at[8])]
    copies += [pltpu.make_async_copy(pq_in.at[i], pq_ref.at[i], sems.at[i]) for i in range(8)]
    for copy in copies:
        copy.start()
    for copy in copies:
        copy.wait()


def per_device(queries, codebook, pq_codes, probes, vectors, cand_owner, cand_row):
    vmem = pl.BlockSpec(memory_space=pltpu.VMEM)
    hbm = pl.BlockSpec(memory_space=pltpu.HBM)
    dma = pltpu.SemaphoreType.DMA
    outs = (
        jax.ShapeDtypeStruct((8, 256, 256), F32),
        jax.ShapeDtypeStruct((8, 16), F32),
    )
    held = pl.pallas_call(
        kernel,
        out_shape=outs,
        in_specs=[hbm] * 7,
        out_specs=(vmem, vmem),
        scratch_shapes=[
            pltpu.VMEM((8, 768), F32),
            pltpu.VMEM((8, 256), I32),
            pltpu.VMEM((8, 16), I32),
            pltpu.VMEM((8, 16), I32),
            pltpu.VMEM((8, 96, 256), I32),
            pltpu.VMEM((96, 8, 256), F32),
            pltpu.VMEM((1024, 768), F32),
            pltpu.VMEM((48, 16, 256), BF16),
            pltpu.VMEM((1024, 768), BF16),
            pltpu.VMEM((8, 768, 256), BF16),
            pltpu.VMEM((2, 4, 4, 2, 16, 384), BF16),
            pltpu.VMEM((8, 16, 384), BF16),
            pltpu.VMEM((8, 16, 128), BF16),
            pltpu.VMEM((128, 128), F32),
            pltpu.VMEM((128, 128), F32),
            pltpu.VMEM((128, 128), F32),
            pltpu.VMEM((16, 1, 128), F32),
            pltpu.VMEM((16, 1, 128), F32),
            pltpu.VMEM((16, 16, 768), BF16),
            pltpu.VMEM((16, 16, 768), BF16),
            pltpu.VMEM((2, 1, 128), F32),
            pltpu.VMEM((128, 1, 128), F32),
            pltpu.VMEM((128, 128), F32),
            dma((7,)),
            pltpu.SemaphoreType.REGULAR,
            dma((8,)), dma((8,)), dma((8,)), dma((8,)),
            dma((2, 3, 4)), dma((2, 3, 4)),
            dma((16,)), dma((16,)), dma((16,)), dma((16,)),
            dma((1,)), dma((1,)),
        ],
        compiler_params=pltpu.CompilerParams(
            vmem_limit_bytes=32 << 20, collective_id=0, has_side_effects=True
        ),
        cost_estimate=pl.CostEstimate(flops=3_000_000_000, bytes_accessed=7_000_000, transcendentals=0),
        name="search",
    )(
        *(
            pltpu.with_memory_space_constraint(operand, pltpu.HBM)
            for operand in (
                queries,
                probes.T,
                cand_owner,
                cand_row,
                pq_codes,
                codebook.transpose(0, 2, 1),
                vectors,
            )
        )
    )
    return pl.pallas_call(
        hand_over,
        out_shape=outs,
        in_specs=[pl.BlockSpec(memory_space=pl.ANY)] * 2,
        out_specs=(hbm, hbm),
        scratch_shapes=[dma((9,))],
        compiler_params=pltpu.CompilerParams(vmem_limit_bytes=16 << 20),
        name="hand_over",
    )(*held)


def solution(mesh):
    both = ("group", "shard")
    in_specs = (
        P(both, None),
        P(),
        P(both, None, None),
        P("group", None),
        P(both, None),
        P(both, None),
        P(both, None),
    )
    out_specs = (P(both, None, None), P(both, None))
    return jax.shard_map(
        per_device, mesh=mesh, in_specs=in_specs, out_specs=out_specs, check_vma=False
    )
```

```python
import jax
import jax.numpy as jnp
from jax import lax
from jax.experimental import pallas as pl
from jax.experimental.pallas import tpu as pltpu
from jax.sharding import PartitionSpec as P

MESH = pl.DeviceIdType.MESH
F32, BF16, I32 = jnp.float32, jnp.bfloat16, jnp.int32
GROUP = 16


def lane_gather(table, index):
    numbers = lax.GatherDimensionNumbers(
        offset_dims=(),
        collapsed_slice_dims=(1,),
        start_index_map=(1,),
        operand_batching_dims=(0,),
        start_indices_batching_dims=(0,),
    )
    return lax.gather(
        table, index[..., None], numbers, (1, 1), mode=lax.GatherScatterMode.PROMISE_IN_BOUNDS
    )


def iota(shape, dim):
    return lax.broadcasted_iota(I32, shape, dim)


def kernel(
    q_hbm,
    probes_hbm,
    owner_hbm,
    row_hbm,
    codes_hbm,
    book_hbm,
    vectors_hbm,
    pq_ref,
    rr_ref,
    q_ref,
    probes_ref,
    owner_ref,
    row_ref,
    codes,
    book,
    vectors,
    book16,
    vectors16,
    decoded,
    group_q,
    cube_q,
    cube_w,
    slot_t,
    place_t,
    row_t,
    want_out,
    want_in,
    slot_out,
    slot_in,
    score_out,
    score_in,
    total,
    load_sem,
    plane_sem,
    cq_s, cq_r, cw_s, cw_r,
    g_s, g_r,
    sq_s, sq_r, sw_s, sw_r,
    rs_s, rs_r,
):
    x = lax.axis_index("group")
    s = lax.axis_index("shard")
    y, z, c = s // 8, (s // 2) % 4, s % 2
    me = x * 32 + s
    a = x * 2 + c
    w = y * 4 + z

    def device(x, y, z, c):
        return {"group": x, "shard": (y * 4 + z) * 2 + c}

    def cube_peer(i):
        p = (a + i) % 8
        return p, device(p // 2, y, z, p % 2)

    def plane_peer(dy, dz):
        to_y, to_z = (y + dy) % 4, (z + dz) % 4
        return to_y * 4 + to_z, device(x, to_y, to_z, c)

    plane_offsets = [(dy, dz) for dy in range(4) for dz in range(4)]
    plane_offsets.sort(key=lambda o: -sum(min(d, 4 - d) for d in o))

    def line_peer(axis, i):
        return (
            device(x, (y + i) % 4, z, c) if axis == 0 else device(x, y, (z + i) % 4, c)
        )

    barrier = pltpu.get_barrier_semaphore()
    for i in (2, 1, 3):
        for axis in range(2):
            pl.semaphore_signal(barrier, inc=1, device_id=line_peer(axis, i), device_id_type=MESH)
    for i in (4, 5, 2, 3, 6, 7, 1):
        pl.semaphore_signal(barrier, inc=1, device_id=cube_peer(i)[1], device_id_type=MESH)

    loads = [
        pltpu.make_async_copy(src, dst, load_sem.at[i])
        for i, (src, dst) in enumerate(
            (
                (q_hbm, q_ref),
                (owner_hbm, owner_ref),
                (row_hbm, row_ref),
                (book_hbm, book),
                (codes_hbm, codes),
                (probes_hbm, probes_ref),
                (vectors_hbm, vectors),
            )
        )
    ]
    for load in loads:
        load.start()

    def remote(src, dst, send, recv, to):
        return pltpu.make_async_remote_copy(
            src_ref=src, dst_ref=dst, send_sem=send, recv_sem=recv, device_id=to, device_id_type=MESH
        )

    for load in loads[:3]:
        load.wait()
    q = q_ref[...]
    high = q.astype(BF16)
    low = (q - high.astype(F32)).astype(BF16)
    cube_q[a] = jnp.concatenate([high[:, :384], high[:, 384:]], axis=0)
    for h in range(2):
        group_q[h, y, z, c] = jnp.concatenate(
            [high[:, h * 384 : h * 384 + 384], low[:, h * 384 : h * 384 + 384]], axis=0
        )
    owner = owner_ref[...]
    row = row_ref[...].astype(F32)
    lanes = iota((8, 128), 1)
    present = jnp.zeros((8, 128), F32)
    wanted = jnp.zeros((8, 128), F32)
    for k in range(16):
        hit = owner[:, k : k + 1] == lanes
        present = jnp.where(hit, 1.0, present)
        wanted = jnp.where(hit, row[:, k : k + 1], wanted)
    earlier = (iota((8, 8), 1) < iota((8, 8), 0)).astype(BF16)
    rank = jnp.dot(earlier, present.astype(BF16), preferred_element_type=F32)
    slot = (a * 2).astype(F32) + rank
    rows = [
        jnp.sum(jnp.where((present > 0.0) & (rank == float(k)), wanted, 0.0), axis=0, keepdims=True)
        for k in range(2)
    ]
    rows = jnp.concatenate(rows + [jnp.zeros((6, 128), F32)], axis=0)
    upper = jnp.floor(rows * (1.0 / 32.0))
    digits = upper + pltpu.roll(rows - upper * 32.0, 2, 0)
    cube_w[a] = jnp.concatenate(
        [jnp.where(present > 0.0, slot, -1.0), digits], axis=0
    ).astype(BF16)
    place_t[...] = jnp.zeros((128, 128), F32)

    pl.semaphore_wait(barrier, 13)

    cube_copies, wish_copies = [], []
    for block, send, recv, copies in (
        (cube_w.at[a], cw_s, cw_r, wish_copies),
        (cube_q.at[a], cq_s, cq_r, cube_copies),
    ):
        for i in (4, 5, 3, 2, 6, 7, 1):
            copy = remote(block, block, send.at[i], recv.at[i], cube_peer(i)[1])
            copy.start()
            copies.append(copy)

    for i in (2, 1, 3):
        pl.semaphore_signal(plane_sem, inc=1, device_id=line_peer(1, i), device_id_type=MESH)

    first_copies, second_copies = [], []
    for i in (1, 3, 2):
        for h in range(2):
            block = group_q.at[h, y, z, c]
            copy = remote(block, block, g_s.at[h, 0, i], g_r.at[h, 0, i], line_peer(h, i))
            copy.start()
            first_copies.append(copy)

    loads[3].wait()

    def to_book16(i, _):
        pair = book[pl.ds(i * 2, 2)]
        book16[i] = jnp.concatenate([pair[0], pair[1]], axis=0).astype(BF16)
        return 0

    lax.fori_loop(0, 48, to_book16, 0, unroll=8)
    loads[4].wait()

    def decode(l, _):
        for m in range(48):
            for h in range(2):
                span = slice(h * 128, h * 128 + 128)
                index = jnp.concatenate(
                    [
                        jnp.broadcast_to(codes[l, 2 * m : 2 * m + 1, span], (8, 128)),
                        jnp.broadcast_to(codes[l, 2 * m + 1 : 2 * m + 2, span], (8, 128)),
                    ],
                    axis=0,
                )
                near = (index & 127).astype(jnp.int16)
                decoded[l, m * 16 : m * 16 + 16, span] = jnp.where(
                    index < 128,
                    lane_gather(book16[m, :, :128], near),
                    lane_gather(book16[m, :, 128:], near),
                )
        return 0

    lax.fori_loop(0, 3, decode, 0)

    for copy in wish_copies:
        copy.wait_recv()
    pl.semaphore_wait(plane_sem, 3)
    codes_in = cube_w[...].astype(F32)
    slot_t[...] = jnp.concatenate(
        [codes_in[:, :8].reshape(64, 128), jnp.full((64, 128), -1.0, F32)], axis=0
    ).T
    for k in range(8):
        pair = codes_in[k, 8:10] * 32.0 + codes_in[k, 10:12]
        place_t[pl.ds(pl.multiple_of(w % 8 * 16, 16), 16), :] += jnp.pad(
            pair, ((2 * k, 14 - 2 * k), (0, 0))
        )
    row_t[...] = place_t[...].T
    slot_copies = []
    for dy, dz in plane_offsets:
        k = dy * 4 + dz
        p, to = plane_peer(dy, dz)
        want_out[k] = row_t[pl.ds(x * 32 + p * 2 + c, 1), :]
        if k == 0:
            want_in[w] = want_out[0]
            continue
        copy = remote(want_out.at[k], want_in.at[w], sw_s.at[k], sw_r.at[k], to)
        copy.start()
        slot_copies.append(copy)
    places = iota((16, 128), 0).astype(F32)
    picks = []
    for dy, dz in plane_offsets:
        p, _ = plane_peer(dy, dz)
        line = jnp.broadcast_to(slot_t[pl.ds(x * 32 + p * 2 + c, 1), :], (16, 128))
        picks.append(jnp.where(line == places, 1.0, 0.0))
    pick_all = jnp.concatenate(picks, axis=0)[:, :64].astype(BF16)
    for copy in cube_copies:
        copy.wait_recv()
    cube = cube_q[...]
    columns = [cube[:, h * 8 : h * 8 + 8, :].reshape(64, 384) for h in range(2)]
    columns = jnp.concatenate(columns, axis=1)
    for first in range(0, 16, GROUP):
        group = plane_offsets[first : first + GROUP]
        pick = pick_all[first * 16 : (first + GROUP) * 16]
        chosen = jnp.dot(pick, columns, preferred_element_type=F32).astype(BF16)
        for n, (dy, dz) in enumerate(group):
            k = dy * 4 + dz
            if k == 0:
                slot_in[w] = chosen[n * 16 : n * 16 + 16]
                continue
            slot_out[k] = chosen[n * 16 : n * 16 + 16]
            _, to = plane_peer(dy, dz)
            copy = remote(slot_out.at[k], slot_in.at[w], sq_s.at[k], sq_r.at[k], to)
            copy.start()
            slot_copies.append(copy)

    lax.fori_loop(3, 8, decode, 0)
    for copy in first_copies:
        copy.wait_recv()
    for i in (1, 3, 2):
        for h in range(2):
            block = group_q.at[h, :, z, c] if h == 0 else group_q.at[h, y, :, c]
            copy = remote(block, block, g_s.at[h, 1, i], g_r.at[h, 1, i], line_peer(1 - h, i))
            copy.start()
            second_copies.append(copy)
    loads[6].wait()

    def to_vectors16(i, _):
        span = pl.ds(pl.multiple_of(i * 128, 128), 128)
        vectors16[span, :] = vectors[span, :].astype(BF16)
        return 0

    lax.fori_loop(0, 8, to_vectors16, 0)

    for copy in slot_copies:
        copy.wait_recv()
    slots = slot_in[...].reshape(256, 768)
    ids = jnp.concatenate(
        [jnp.sum(want_in[b * 8 : b * 8 + 8], axis=0) for b in range(2)], axis=1
    ).astype(I32)
    found = jnp.zeros((256, 256), F32)
    for b in range(4):
        part = lax.dot_general(
            vectors16[b * 256 : b * 256 + 256, :],
            slots,
            (((1,), (1,)), ((), ())),
            preferred_element_type=F32,
        )
        found = jnp.where(iota((256, 256), 0) + b * 256 == ids, part, found)
    scored = jnp.sum(found, axis=0, keepdims=True)
    for b in range(2):
        score_out[b] = scored[:, b * 128 : b * 128 + 128]
    score_in[me] = score_out[w // 8]
    offsets = [(dx, dy, dz, dc) for dx in range(4) for dy in range(4) for dz in range(4) for dc in range(2)]
    offsets.sort(key=lambda o: -sum(min(d, 4 - d) for d in o[:3]))
    offsets.remove((0, 0, 0, 0))
    for dx, dy, dz, dc in offsets:
        p = (y + dy) % 4 * 4 + (z + dz) % 4
        to = {"group": (x + dx) % 4, "shard": p * 2 + (c + dc) % 2}
        remote(score_out.at[p // 8], score_in.at[me], rs_s.at[0], rs_r.at[0], to).start()

    for copy in second_copies:
        copy.wait_recv()
    sibling = device(x, y, z, 1 - c)
    core_copies = []
    for h in range(2):
        block = group_q.at[h, :, :, c]
        copy = remote(block, block, g_s.at[h, 2, 0], g_r.at[h, 2, 0], sibling)
        copy.start()
        core_copies.append(copy)
    for copy in core_copies:
        copy.wait_recv()

    loads[5].wait()
    probes = probes_ref[...]

    def score_list(l, _):
        left = jnp.concatenate(
            [group_q[0].reshape(512, 384), group_q[1].reshape(512, 384)], axis=1
        )
        both = jnp.dot(left, decoded[l], preferred_element_type=F32).reshape(32, 2, 8, 256)
        sums = (both[:, 0] + both[:, 1]).reshape(256, 256)
        probed = jnp.max(jnp.where(probes == s * 8 + l, 1.0, 0.0), axis=0, keepdims=True)
        pq_ref[l] = jnp.where(probed > 0.0, sums.T, 0.0)
        return 0

    lax.fori_loop(0, 8, score_list, 0, unroll=2)

    everyone = score_in.at[pl.ds(0, 127)]
    pltpu.make_async_copy(everyone, everyone, rs_r.at[0]).wait()
    total[...] = score_in[...].reshape(128, 128).T
    line = w % 8 * 16 + a * 2
    own = jnp.where(rank < 0.5, total[pl.ds(line, 1), :], total[pl.ds(line + 1, 1), :])
    result = jnp.zeros((8, 16), F32)
    for k in range(16):
        value = jnp.sum(
            jnp.where(owner[:, k : k + 1] == lanes, own, 0.0), axis=1, keepdims=True
        )
        result = jnp.where(iota((8, 16), 1) == k, value, result)
    rr_ref[...] = result

    for copy in (
        wish_copies + cube_copies + first_copies + second_copies + core_copies + slot_copies
    ):
        copy.wait_send()
    pltpu.make_async_copy(everyone, everyone, rs_s.at[0]).wait()


def hand_over(pq_in, rr_in, pq_ref, rr_ref, sems):
    copies = [pltpu.make_async_copy(rr_in, rr_ref, sems.at[8])]
    copies += [pltpu.make_async_copy(pq_in.at[i], pq_ref.at[i], sems.at[i]) for i in range(8)]
    for copy in copies:
        copy.start()
    for copy in copies:
        copy.wait()


def per_device(queries, codebook, pq_codes, probes, vectors, cand_owner, cand_row):
    vmem = pl.BlockSpec(memory_space=pltpu.VMEM)
    hbm = pl.BlockSpec(memory_space=pltpu.HBM)
    dma = pltpu.SemaphoreType.DMA
    outs = (
        jax.ShapeDtypeStruct((8, 256, 256), F32),
        jax.ShapeDtypeStruct((8, 16), F32),
    )
    held = pl.pallas_call(
        kernel,
        out_shape=outs,
        in_specs=[hbm] * 7,
        out_specs=(vmem, vmem),
        scratch_shapes=[
            pltpu.VMEM((8, 768), F32),
            pltpu.VMEM((8, 256), I32),
            pltpu.VMEM((8, 16), I32),
            pltpu.VMEM((8, 16), I32),
            pltpu.VMEM((8, 96, 256), I32),
            pltpu.VMEM((96, 8, 256), F32),
            pltpu.VMEM((1024, 768), F32),
            pltpu.VMEM((48, 16, 256), BF16),
            pltpu.VMEM((1024, 768), BF16),
            pltpu.VMEM((8, 768, 256), BF16),
            pltpu.VMEM((2, 4, 4, 2, 16, 384), BF16),
            pltpu.VMEM((8, 16, 384), BF16),
            pltpu.VMEM((8, 16, 128), BF16),
            pltpu.VMEM((128, 128), F32),
            pltpu.VMEM((128, 128), F32),
            pltpu.VMEM((128, 128), F32),
            pltpu.VMEM((16, 1, 128), F32),
            pltpu.VMEM((16, 1, 128), F32),
            pltpu.VMEM((16, 16, 768), BF16),
            pltpu.VMEM((16, 16, 768), BF16),
            pltpu.VMEM((2, 1, 128), F32),
            pltpu.VMEM((128, 1, 128), F32),
            pltpu.VMEM((128, 128), F32),
            dma((7,)),
            pltpu.SemaphoreType.REGULAR,
            dma((8,)), dma((8,)), dma((8,)), dma((8,)),
            dma((2, 3, 4)), dma((2, 3, 4)),
            dma((16,)), dma((16,)), dma((16,)), dma((16,)),
            dma((1,)), dma((1,)),
        ],
        compiler_params=pltpu.CompilerParams(
            vmem_limit_bytes=32 << 20, collective_id=0, has_side_effects=True
        ),
        cost_estimate=pl.CostEstimate(flops=3_000_000_000, bytes_accessed=7_000_000, transcendentals=0),
        name="search",
    )(
        *(
            pltpu.with_memory_space_constraint(operand, pltpu.HBM)
            for operand in (
                queries,
                probes.T,
                cand_owner,
                cand_row,
                pq_codes,
                codebook.transpose(0, 2, 1),
                vectors,
            )
        )
    )
    return pl.pallas_call(
        hand_over,
        out_shape=outs,
        in_specs=[pl.BlockSpec(memory_space=pl.ANY)] * 2,
        out_specs=(hbm, hbm),
        scratch_shapes=[dma((9,))],
        compiler_params=pltpu.CompilerParams(vmem_limit_bytes=16 << 20),
        name="hand_over",
    )(*held)


def solution(mesh):
    both = ("group", "shard")
    in_specs = (
        P(both, None),
        P(),
        P(both, None, None),
        P("group", None),
        P(both, None),
        P(both, None),
        P(both, None),
    )
    out_specs = (P(both, None, None), P(both, None))
    return jax.shard_map(
        per_device, mesh=mesh, in_specs=in_specs, out_specs=out_specs, check_vma=False
    )
```
